128 devices in a mesh: seq: 8 (over y_lo, z), chan: 16 (over x, y_hi, core).
Axes of the slice: x: 4, y: 4 (y_hi: 2, y_lo: 2; y = y_hi * 2 + y_lo), z: 4, core: 2. Of those that a mesh axis runs over, the one named last changes fastest.
Arguments:
- hidden: bfloat16 [8192, 8192], P('seq', 'chan'), may hold values from -6 to 6
- in_weights: bfloat16 [8192, 24576], P(('seq', 'chan')), may hold values from -0.0625 to 0.0625
- filter_bank: float32 [7, 512], replicated, may hold values from -3 to 3
- assignment: int32 [512], P('chan'), may hold values from 0 to 511, each once
Outputs:
- hyena_out: bfloat16 [8192, 8192], P('seq', 'chan')
The draws below stay inside these ranges and needn't reach their ends.
Inputs may be any that keep to these rules, and one draw needn't show every extreme that they name: `assignment`: a permutation: every filter is used by exactly one group.
All inputs are finite; a program needn't handle non-finite values.
Results may differ from the reference program's by a relative error of at most 0.001.
Values may be sent and summed in bfloat16 or wider, within the bound.
A program may use at most 128 MiB of HBM per device.

```python
import jax
import jax.numpy as jnp

D = 8192
GROUP = 16
TAPS = 7
FILTERS = 512
TOKENS = 8192


def levels(stream_key, extent, shards, least, largest):
    def one(position, blocks):
        heights = jax.random.uniform(jax.random.fold_in(jax.random.fold_in(stream_key, 6), position), (blocks,), jnp.float32, least / len(shards), largest / len(shards))
        return jnp.repeat(jnp.exp(heights), extent[position] // blocks).reshape((-1,) + (1,) * (len(extent) - position - 1))

    loudness = one(*shards[0])
    for cut in shards[1:]:
        loudness = loudness * one(*cut)
    return loudness


def gaussian(rng, dims, spread, limit, pieces=(), dtype=jnp.bfloat16):
    array = spread * jax.random.normal(rng, dims, jnp.float32)
    if pieces:
        array = array * levels(rng, dims, pieces, -0.22, 0.18)
    return jnp.clip(array, -limit, limit).astype(dtype)


def setup_inputs(seed: int = 0) -> dict:
    key_list = jax.random.split(jax.random.key(seed), 5)
    return {
        "hidden": gaussian(key_list[0], (TOKENS, D), 1.0, 6.0, ((0, 8), (1, 16))),
        "in_weights": gaussian(key_list[1], (D, 3 * D), D ** -0.5, 0.0625, ((0, 128),)),
        "filter_bank": gaussian(key_list[2], (TAPS, FILTERS), 0.5, 3.0, (), jnp.float32),
        "assignment": jax.random.permutation(key_list[3], FILTERS).astype(jnp.int32),
    }


def reference(hidden, in_weights, filter_bank, assignment):
    chosen = jnp.take(filter_bank, assignment, axis=1)
    filter_taps = jnp.repeat(chosen, GROUP, axis=1)
    query = jnp.dot(hidden, in_weights[:, :D], preferred_element_type=jnp.float32)
    keyed = jnp.dot(hidden, in_weights[:, D:2 * D], preferred_element_type=jnp.float32)
    valued = jnp.dot(hidden, in_weights[:, 2 * D:], preferred_element_type=jnp.float32)
    product = keyed * valued
    padded = jnp.concatenate([jnp.zeros((TAPS - 1, D), jnp.float32), product], axis=0)
    filtered = jnp.zeros((TOKENS, D), jnp.float32)
    for lag_index in range(TAPS):
        begin = TAPS - 1 - lag_index
        filtered = filtered + filter_taps[lag_index][None, :] * padded[begin:begin + TOKENS]
    return (query * filtered).astype(jnp.bfloat16)
```

```python
import jax
import jax.numpy as jnp
from jax import lax
from jax.experimental import pallas as pl
from jax.experimental.pallas import tpu as pltpu
from jax.sharding import PartitionSpec as P

D = 8192
GROUP = 16
TAPS = 7
FILTERS = 512
TOKENS = 1024
WIDTH = 512
ROWS = 64
CHUNK = 256
CHUNKS = TOKENS // CHUNK
MESH = pl.DeviceIdType.MESH

ROUND_ROWS = (3, 0, 1, 2)


def device(x, y, z, core):
    return ((y % 2) * 4 + z, x * 4 + (y // 2) * 2 + core)


def kernel(hidden, weights, bank, assigned, out, hbuf, wbuf, acc, prod, stage, taps, bank8,
           hsem, wsem, sibsem, misc, send):
    seq, chan = lax.axis_index("seq"), lax.axis_index("chan")
    x, y, z, core = chan // 4, (chan // 2 % 2) * 2 + seq // 4, seq % 4, chan % 2
    y_hi, y_lo = y // 2, y % 2
    across = (y_lo + core) % 2
    left, right = (x + 3) % 4, (x + 1) % 4
    down, up = (y + 3) % 4, (y + 1) % 4
    below, above = (z + 3) % 4, (z + 1) % 4
    sibling = device(x, y, z, 1 - core)
    partner = device(x, y + 1 - 2 * y_lo, z, 1 - core)
    x_to = {1: device(right, y, z, core), -1: device(left, y, z, core)}
    y_to = {1: device(x, up, z, core), -1: device(x, down, z, core)}
    z_to = {1: device(x, y, above, core), -1: device(x, y, below, core)}

    def xor(a, bits):
        low, high = a % 2, a // 2
        low = 1 - low if bits & 1 else low
        high = 1 - high if bits & 2 else high
        return high * 2 + low

    mates = []
    for i in range(16):
        mates.append((xor(x, i & 3), xor(y, ((i >> 2) & 1) * 2 + (i >> 3))))

    def copy(src, dst, send_sem, recv_sem, to):
        return pltpu.make_async_remote_copy(
            src_ref=src, dst_ref=dst, send_sem=send_sem, recv_sem=recv_sem,
            device_id=to, device_id_type=MESH)

    def rows_of(piece, owner):
        return pl.ds(pl.multiple_of((piece * 2 + owner) * ROWS, ROWS), ROWS)

    def piece_of(xs, ys, zs):
        return ((ys % 2) * 4 + zs) * 8 + xs * 2 + ys // 2

    def w_send(piece, to, sem):
        ref = wbuf.at[:, rows_of(piece, core), :]
        copy(ref, ref, send.at[sem], wsem.at[piece], to).start()

    def w_sib(piece, group):
        ref = wbuf.at[:, rows_of(piece, core), :]
        copy(ref, ref, send.at[2], sibsem.at[group], sibling).start()

    def w_wait(piece):
        ref = wbuf.at[:, rows_of(piece, core), :]
        copy(ref, ref, send.at[0], wsem.at[piece], sibling).wait_recv()

    def sib_wait(group):
        ref = wbuf.at[:, pl.ds(0, 8 * ROWS), :]
        copy(ref, ref, send.at[2], sibsem.at[group], sibling).wait_recv()

    def block(xs, yh, ks):
        return xs * 4 + yh * 2 + ks

    def h_ref(b, r):
        return hbuf.at[b, pl.ds(ROUND_ROWS[r] * CHUNK, CHUNK), :]

    def h_send(b, r, to, sem):
        copy(h_ref(b, r), h_ref(b, r), send.at[sem], hsem.at[b * CHUNKS + r], to).start()

    def h_x(b, r, sides=(1, -1)):
        for side in sides:
            h_send(b, r, x_to[side], 3)

    def h_y(b, r, sides=(1, -1)):
        for side in sides:
            h_send(b, r, y_to[side], 4)

    def h_wait(b, r):
        copy(h_ref(b, r), h_ref(b, r), send.at[3], hsem.at[b * CHUNKS + r], sibling).wait_recv()

    own_block = block(x, y_hi, core)
    own_piece = piece_of(x, y, z)
    my_group = x * 4 + y

    def local_hidden(r):
        rows = pl.ds(ROUND_ROWS[r] * CHUNK, CHUNK)
        return pltpu.make_async_copy(hidden.at[rows, :], h_ref(own_block, r),
                                     hsem.at[own_block * CHUNKS + r])

    def local_weights(part):
        return pltpu.make_async_copy(
            weights.at[:, pl.ds(pl.multiple_of(part * D + my_group * WIDTH, WIDTH), WIDTH)],
            wbuf.at[part, rows_of(own_piece, core), :], misc.at[2 + part])

    for part in range(3):
        local_weights(part).start()

    @pl.when(across == 0)
    def _():
        for r in range(CHUNKS):
            local_hidden(r).start()

    barrier = pltpu.get_barrier_semaphore()
    greeted = [device(mx, my, z, core) for mx, my in mates[1:]]
    greeted += [z_to[1], z_to[-1], sibling, partner,
                device(x, y, above, 1 - core), device(x, y, below, 1 - core)]
    for to in greeted:
        pl.semaphore_signal(barrier, inc=1, device_id=to, device_id_type=MESH)
    pl.semaphore_wait(barrier, len(greeted))

    def all_to_all(i):
        mx, my = mates[i]
        to = device(mx, my, z, core)
        for part in range(3):
            column = pl.multiple_of(part * D + (mx * 4 + my) * WIDTH, WIDTH)
            copy(weights.at[:, pl.ds(column, WIDTH)], wbuf.at[part, rows_of(own_piece, core), :],
                 send.at[0], wsem.at[own_piece], to).start()

    @pl.when(across == 1)
    def _():
        for r in range(CHUNKS):
            rows = pl.ds(ROUND_ROWS[r] * CHUNK, CHUNK)
            copy(hidden.at[rows, :], h_ref(own_block, r), send.at[5],
                 hsem.at[own_block * CHUNKS + r], sibling).start()

    for i in range(1, 16):
        all_to_all(i)

    def own_weights(i):
        mx, my = mates[i]
        piece = piece_of(mx, my, z)
        if i == 0:
            for part in range(3):
                local_weights(part).wait()
        else:
            w_wait(piece)
        w_send(piece, z_to[1], 1)
        w_send(piece, z_to[-1], 1)
        w_sib(piece, i >> 3)

    def near_weights(i):
        mx, my = mates[i]
        piece = piece_of(mx, my, below)
        w_wait(piece)
        if i % 2 == 0:
            w_send(piece, z_to[1], 1)
        w_sib(piece, 2 + (i >> 3))
        piece = piece_of(mx, my, above)
        w_wait(piece)
        if i % 2 == 1:
            w_send(piece, z_to[-1], 1)
        w_sib(piece, 4 + (i >> 3))

    def far_weights(i):
        mx, my = mates[i]
        piece = piece_of(mx, my, (z + 2) % 4)
        w_wait(piece)
        w_sib(piece, 6 + (i >> 3))

    yh_down, yh_up = down // 2, up // 2

    def hidden0(r):
        @pl.when(across == 0)
        def _():
            a, b = block(x, y_hi, 0), block(x, y_hi, 1)
            h_wait(a, r)
            h_x(a, r)
            h_y(a, r)
            h_wait(b, r)
            h_y(b, r)
            h_x(b, r)

    def hidden1(r):
        @pl.when(across == 0)
        def _():
            a = block(left, y_hi, 0)
            h_wait(a, r)
            if r % 2 == 0:
                h_x(a, r, (1,))
            h_y(a, r)
            a = block(right, y_hi, 0)
            h_wait(a, r)
            if r % 2 == 1:
                h_x(a, r, (-1,))
            h_y(a, r)

        @pl.when(across == 1)
        def _():
            b = block(x, yh_down, 1)
            h_wait(b, r)
            if r % 2 == 0:
                h_y(b, r, (1,))
            h_x(b, r)
            b = block(x, yh_up, 1)
            h_wait(b, r)
            if r % 2 == 1:
                h_y(b, r, (-1,))
            h_x(b, r)

    def hidden2(r):
        @pl.when(across == 0)
        def _():
            a = block((x + 2) % 4, y_hi, 0)
            h_wait(a, r)
            h_y(a, r)
            b = block(x, 1 - y_hi, 1)
            h_wait(b, r)
            h_x(b, r)

    def hidden3(r):
        @pl.when(across == 1)
        def _():
            for m, xs in enumerate((x, left, right, (x + 2) % 4)):
                a = block(xs, yh_down, 0)
                h_wait(a, r)
                if (m + r) % 2 == 0:
                    h_y(a, r, (1,))
                a = block(xs, yh_up, 0)
                h_wait(a, r)
                if (m + r) % 2 == 1:
                    h_y(a, r, (-1,))

        for yh in range(2):
            b = block(left, yh, 1)
            h_wait(b, r)
            if (yh + r) % 2 == 0:
                h_x(b, r, (1,))
            b = block(right, yh, 1)
            h_wait(b, r)
            if (yh + r) % 2 == 1:
                h_x(b, r, (-1,))

    def hidden4(r):
        @pl.when(across == 0)
        def _():
            for xs in (x, left, right, (x + 2) % 4):
                h_wait(block(xs, 1 - y_hi, 0), r)

        for yh in range(2):
            h_wait(block((x + 2) % 4, yh, 1), r)

    def make_taps():
        bank8[0:TAPS, :] = bank[...]
        bank8[TAPS:, :] = jnp.zeros((8 - TAPS, FILTERS), jnp.float32)

        @pl.when(across == 0)
        def _():
            filters = lax.broadcasted_iota(jnp.int32, (FILTERS, WIDTH), 0)
            selector = (filters == assigned[...]).astype(jnp.float32)
            taps[...] = jnp.dot(bank8[...], selector, precision=lax.Precision.HIGHEST,
                                preferred_element_type=jnp.float32)
            copy(taps, taps, send.at[6], misc.at[0], sibling).start()

        @pl.when(across == 1)
        def _():
            copy(taps, taps, send.at[6], misc.at[0], sibling).wait_recv()

        prod[0:8, :] = jnp.zeros((8, WIDTH), jnp.float32)

    def dot(s):
        m = jnp.where(s < 12, s % 6, jnp.where(s < 16, s % 2, s % 8))
        r = jnp.where(s < 12, s // 6, jnp.where(s < 16, (s - 12) // 2, s // 8))
        hop = m // 2
        hop = jnp.where(s < 12, hop + hop // 2, 2)
        z_block = ((y_lo + m) % 2) * 4 + (z + hop) % 4
        step = m // 2
        step = jnp.where(step == 2, 3, jnp.where(step == 3, 2, step))
        x_block = ((x + step) % 4) * 2 + m % 2
        b = jnp.where(s < 16, z_block, x_block)
        rows = jnp.where(r == 0, 3, r - 1) * CHUNK
        rows = pl.ds(pl.multiple_of(rows, CHUNK), CHUNK)
        k0 = pl.ds(pl.multiple_of(b * 1024, 1024), 512)
        k1 = pl.ds(pl.multiple_of(b * 1024 + 512, 512), 512)
        for part in range(3):
            term = jnp.dot(hbuf[2 * b, rows, :], wbuf[part, k0, :],
                           preferred_element_type=jnp.float32)
            term += jnp.dot(hbuf[2 * b + 1, rows, :], wbuf[part, k1, :],
                            preferred_element_type=jnp.float32)
            acc[rows, part * WIDTH:(part + 1) * WIDTH] += term

    SUB = 32

    def products(base):
        def step(i, _):
            rows = pl.ds(pl.multiple_of(base + i * SUB, SUB), SUB)
            prod[pl.ds(pl.multiple_of(base + i * SUB + 8, 8), SUB), :] = (
                acc[rows, WIDTH:2 * WIDTH] * acc[rows, 2 * WIDTH:])
            return 0
        lax.fori_loop(0, CHUNK // SUB, step, 0)

    def filtered(base, count, size):
        def step(i, _):
            first = pl.multiple_of(base + i * size, size)
            near = prod[pl.ds(first, size + 8), :]
            total = jnp.zeros((size, WIDTH), jnp.float32)
            for j in range(TAPS):
                total = total + taps[j:j + 1, :] * near[8 - j:8 - j + size, :]
            rows = pl.ds(first, size)
            stage[rows, :] = (acc[rows, 0:WIDTH] * total).astype(jnp.bfloat16)
            return 0
        lax.fori_loop(0, count, step, 0)

    def out_send(first, count, sem):
        src, dst = stage.at[pl.ds(first, count), :], out.at[pl.ds(first, count), :]

        @pl.when(across == 0)
        def _():
            pltpu.make_async_copy(src, dst, misc.at[sem]).start()

        @pl.when(across == 1)
        def _():
            copy(src, dst, send.at[8], misc.at[sem], partner).start()

    def out_wait(first, count, sem):
        src, dst = stage.at[pl.ds(first, count), :], out.at[pl.ds(first, count), :]

        @pl.when(across == 0)
        def _():
            pltpu.make_async_copy(src, dst, misc.at[sem]).wait()

        @pl.when(across == 1)
        def _():
            copy(src, dst, send.at[8], misc.at[sem], partner).wait_recv()

    halo_from, halo_to = prod.at[pl.ds(TOKENS, 8), :], prod.at[pl.ds(0, 8), :]
    last_window = (z == 3) & (core == 1)
    first_window = (z == 0) & (core == 0)
    next_core = jnp.where(z == 3, 1 - core, core)

    def halo():
        return copy(halo_from, halo_to, send.at[7], misc.at[1], device(x, y, above, next_core))

    def epilogue0():
        products(3 * CHUNK)

        @pl.when(jnp.logical_not(last_window))
        def _():
            halo().start()

        filtered(3 * CHUNK + 32, 7, 32)
        out_send(3 * CHUNK + 32, CHUNK - 32, 5)

    def epilogue1():
        products(0)

        @pl.when(jnp.logical_not(first_window))
        def _():
            halo().wait_recv()

        filtered(0, 8, 32)
        out_send(0, CHUNK, 6)

    def epilogue2():
        products(CHUNK)
        filtered(CHUNK, 8, 32)
        out_send(CHUNK, CHUNK, 7)

    def epilogue3():
        products(2 * CHUNK)
        filtered(2 * CHUNK, 9, 32)
        out_send(2 * CHUNK, CHUNK + 32, 8)

    when, run = {}, {}

    def plan(key, time, fn):
        when[key], run[key] = time, fn

    plan("taps", 3.0, make_taps)
    for i in range(16):
        plan(("own", i), 4 + 3.2 * i, lambda i=i: own_weights(i))
        plan(("near", i), max(50, 10 + 4.2 * i), lambda i=i: near_weights(i))
        plan(("far", i), 70 + 4.2 * (i // 2 + 1), lambda i=i: far_weights(i))
    for r in range(CHUNKS):
        for index, (offset, fn) in enumerate(
                ((0, hidden0), (8, hidden1), (14, hidden2), (20, hidden3), (28, hidden4))):
            plan(("hidden", index, r), 8 + 23 * r + offset, lambda fn=fn, r=r: fn(r))
    for group in range(8):
        members = [("own", "near", "near", "far")[group // 2]]
        last = max(when[members[0], i] for i in range(8 * (group % 2), 8 * (group % 2) + 8))
        plan(("sib", group), last + 4, lambda group=group: sib_wait(group))

    def needs(s):
        r = s // 6 if s < 12 else (s - 12) // 2 if s < 16 else s // 8
        keys = [("hidden", index, r) for index in range(5)]
        if s < 12:
            kinds = [(("own", 0), ("near", 4), ("near", 2))[s % 6 // 2]]
            halves = [s % 2]
        else:
            kinds = [("own", 0), ("near", 4), ("near", 2), ("far", 6)]
            halves = [0, 1]
        for kind, group in kinds:
            for half in halves:
                keys += [(kind, i) for i in range(8 * half, 8 * half + 8)]
                keys.append(("sib", group + half))
        return keys

    before = [[] for _ in range(32)]
    placed = set()
    clock = 0.0
    for s in range(32):
        clock = max([clock + 1.25] + [when[key] for key in needs(s)])
        ready = [key for key in when if when[key] <= clock and key not in placed]
        for key in sorted(ready, key=when.get):
            placed.add(key)
            before[s].append(run[key])
        if s in (16, 17, 24):
            before[s].append({16: epilogue0, 17: epilogue1, 24: epilogue2}[s])
    assert len(placed) == len(when)

    def zero(i, _):
        acc[pl.ds(pl.multiple_of(i * 32, 32), 32), :] = jnp.zeros((32, 3 * WIDTH), jnp.float32)
        return 0
    lax.fori_loop(0, TOKENS // 32, zero, 0)

    def slot_step(s, _):
        for k in range(32):
            if before[k]:
                @pl.when(s == k)
                def _(k=k):
                    for fn in before[k]:
                        fn()
        dot(s)
        return 0
    lax.fori_loop(0, 32, slot_step, 0)
    epilogue3()

    out_wait(3 * CHUNK + 32, CHUNK - 32, 5)
    out_wait(0, CHUNK, 6)
    out_wait(CHUNK, CHUNK, 7)
    out_wait(2 * CHUNK, CHUNK + 32, 8)

    def sent(ref, sem):
        copy(ref, ref, send.at[sem], misc.at[0], sibling).wait_send()

    sent(wbuf.at[:, pl.ds(0, 15 * ROWS), :], 0)
    sent(wbuf.at[:, pl.ds(0, 48 * ROWS), :], 1)
    sent(wbuf.at[:, pl.ds(0, 64 * ROWS), :], 2)

    @pl.when(across == 0)
    def _():
        sent(hbuf.at[pl.ds(0, 9)], 3)
        sent(hbuf.at[pl.ds(0, 10)], 4)
        sent(taps, 6)

    @pl.when(across == 1)
    def _():
        sent(hbuf.at[pl.ds(0, 6)], 3)
        sent(hbuf.at[pl.ds(0, 5)], 4)
        sent(hidden, 5)
        sent(stage, 8)

    @pl.when(jnp.logical_not(last_window))
    def _():
        halo().wait_send()


def on_device(hidden, in_weights, filter_bank, assignment):
    assigned = jnp.repeat(assignment, GROUP)[None, :]
    any_space = pl.BlockSpec(memory_space=pl.ANY)
    vmem = pl.BlockSpec(memory_space=pltpu.VMEM)
    return pl.pallas_call(
        kernel,
        name="hyena",
        out_shape=jax.ShapeDtypeStruct((TOKENS, WIDTH), jnp.bfloat16),
        in_specs=[any_space, any_space, vmem, vmem],
        out_specs=any_space,
        scratch_shapes=[
            pltpu.VMEM((16, TOKENS, WIDTH), jnp.bfloat16),
            pltpu.VMEM((3, D, WIDTH), jnp.bfloat16),
            pltpu.VMEM((TOKENS, 3 * WIDTH), jnp.float32),
            pltpu.VMEM((TOKENS + 8, WIDTH), jnp.float32),
            pltpu.VMEM((TOKENS, WIDTH), jnp.bfloat16),
            pltpu.VMEM((8, WIDTH), jnp.float32),
            pltpu.VMEM((8, FILTERS), jnp.float32),
            pltpu.SemaphoreType.DMA((16 * CHUNKS,)),
            pltpu.SemaphoreType.DMA((64,)),
            pltpu.SemaphoreType.DMA((8,)),
            pltpu.SemaphoreType.DMA((9,)),
            pltpu.SemaphoreType.DMA((9,)),
        ],
        compiler_params=pltpu.CompilerParams(
            collective_id=0, has_side_effects=True, vmem_limit_bytes=60 * 2**20),
        cost_estimate=pl.CostEstimate(
            flops=2 * TOKENS * D * 3 * WIDTH, bytes_accessed=44 * 2**20, transcendentals=0),
    )(hidden, in_weights, filter_bank, assigned)


def solution(mesh):
    in_specs = (P("seq", "chan"), P(("seq", "chan"), None), P(), P("chan"))
    return jax.shard_map(
        on_device, mesh=mesh, in_specs=in_specs, out_specs=P("seq", "chan"), check_vma=False)
```

```python
import jax
import jax.numpy as jnp
from jax import lax
from jax.experimental import pallas as pl
from jax.experimental.pallas import tpu as pltpu
from jax.sharding import PartitionSpec as P

D = 8192
GROUP = 16
TAPS = 7
FILTERS = 512
TOKENS = 1024
WIDTH = 512
ROWS = 64
CHUNK = 256
CHUNKS = TOKENS // CHUNK
MESH = pl.DeviceIdType.MESH

ROUND_ROWS = (3, 0, 1, 2)
ORDER = ((0, 0), (1, 0), (3, 0), (0, 2), (2, 0), (1, 2), (3, 2), (2, 2),
         (0, 1), (0, 3), (1, 1), (3, 3), (1, 3), (3, 1), (2, 1), (2, 3))
FIRST, AFTER = 8.0, 16.0
STAGES = (0.0, 12.0, 24.0, 36.0, 50.0)
LAST = (0.0, 12.0, 24.0, 36.0, 50.0)
SPREAD = (0.1, 0.1)
SPLIT = 6.0
ALL = (3.0, 0.5)
OWN = (4.0, 3.2)
NEAR = (50.0, 10.0, 4.2)
FAR = (70.0, 4.2)
DOT = 1.25

HOPS = (0, 1, 3, 2)
DOTS = tuple(("z", r, hop, half) for r in range(3) for hop in HOPS[:3] for half in range(2))
DOTS += tuple(("z", r, 2, half) for half in range(2) for r in range(3))
DOTS += tuple(("x", 3, step, y_hi) for step in range(4) for y_hi in range(2))


def hidden_needs(m, r):
    return [("h3a", m, r), ("h4a", m, r)] + [
        [("h1", r), ("h2", r)], [("h1", r), ("h3b", r)], [("h1", r), ("h3b", r)],
        [("h2", r), ("h4b", r)]][m]


def timeline():
    when = {("taps",): 30.0, ("zero",): 33.0}
    for i in range(16):
        if i:
            when["all", i] = ALL[0] + ALL[1] * i
        when["own", i] = OWN[0] + OWN[1] * i
        when["near", i] = max(NEAR[0], NEAR[1] + NEAR[2] * i)
        when["far", i] = FAR[0] + FAR[1] * (i // 2 + 1)
    for r in range(CHUNKS):
        start = FIRST + AFTER * r
        stages = STAGES if r < CHUNKS - 1 else LAST
        when["h0b", r] = start + stages[0] + SPLIT
        for index in range(3):
            when["h%d" % index, r] = start + stages[index]
        for m in range(4):
            when["h3a", m, r] = start + stages[3] + SPREAD[0] * m
            when["h4a", m, r] = start + stages[4] + SPREAD[1] * m
        when["h3b", r] = start + stages[3] + SPREAD[0] * 1.5
        when["h4b", r] = start + stages[4] + SPREAD[1] * 2.5
    kinds = {0: "own", 1: "near", 3: "near", 2: "far"}
    for hop in HOPS:
        for half in range(2):
            last = max(when[kinds[hop], i] for i in range(16) if ORDER[i][1] % 2 == half)
            when["sib", hop, half] = last + 3.0

    slots, placed, clock = [], set(), 0.0
    names = list(when)
    for kind, r, step, half in DOTS:
        if kind == "z":
            needs = [key for m in range(4) for key in hidden_needs(m, r)] + [("sib", step, half)]
        else:
            needs = hidden_needs(step, r) + [("sib", hop, h) for hop in HOPS for h in range(2)]
        clock = max([clock + DOT] + [when[key] for key in needs])
        ready = [key for key in names if when[key] <= clock and key not in placed]
        ready = sorted(ready, key=when.get)
        placed.update(ready)
        slots.append(ready)
    rest = [key for key in names if key not in placed]
    assert not rest
    return slots


def device(x, y, z, core):
    return ((y % 2) * 4 + z, x * 4 + (y // 2) * 2 + core)


def kernel(hidden, weights, bank, assigned, out, hbuf, wbuf, acc, prod, stage, taps, bank8,
           hsem, wsem, sibsem, misc, send):
    seq, chan = lax.axis_index("seq"), lax.axis_index("chan")
    x, y, z, core = chan // 4, (chan // 2 % 2) * 2 + seq // 4, seq % 4, chan % 2
    y_hi, y_lo = y // 2, y % 2
    across = (y_lo + core) % 2
    left, right = (x + 3) % 4, (x + 1) % 4
    down, up = (y + 3) % 4, (y + 1) % 4
    below, above = (z + 3) % 4, (z + 1) % 4
    sibling = device(x, y, z, 1 - core)
    partner = device(x, y + 1 - 2 * y_lo, z, 1 - core)
    x_to = {1: device(right, y, z, core), -1: device(left, y, z, core)}
    y_to = {1: device(x, up, z, core), -1: device(x, down, z, core)}
    z_to = {1: device(x, y, above, core), -1: device(x, y, below, core)}

    sign = 1 - 2 * core
    mates_to = [((x + sign * dx + 4) % 4, (y + sign * dy + 4) % 4) for dx, dy in ORDER]
    mates = [((x - sign * dx + 4) % 4, (y - sign * dy + 4) % 4) for dx, dy in ORDER]

    def copy(src, dst, send_sem, recv_sem, to):
        return pltpu.make_async_remote_copy(
            src_ref=src, dst_ref=dst, send_sem=send_sem, recv_sem=recv_sem,
            device_id=to, device_id_type=MESH)

    def rows_of(piece, owner):
        return pl.ds(pl.multiple_of((piece * 2 + owner) * ROWS, ROWS), ROWS)

    def piece_of(xs, ys, zs):
        return ((ys % 2) * 4 + zs) * 8 + xs * 2 + ys // 2

    def w_send(piece, to, sem):
        ref = wbuf.at[:, rows_of(piece, core), :]
        copy(ref, ref, send.at[sem], wsem.at[piece], to).start()

    def w_sib(piece, group):
        ref = wbuf.at[:, rows_of(piece, core), :]
        copy(ref, ref, send.at[2], sibsem.at[group], sibling).start()

    def w_wait(piece):
        ref = wbuf.at[:, rows_of(piece, core), :]
        copy(ref, ref, send.at[0], wsem.at[piece], sibling).wait_recv()

    def sib_wait(hop, half):
        ref = wbuf.at[:, pl.ds(0, 8 * ROWS), :]
        copy(ref, ref, send.at[2], sibsem.at[2 * hop + half], sibling).wait_recv()

    def block(xs, yh, ks):
        return xs * 4 + yh * 2 + ks

    def h_ref(b, r):
        return hbuf.at[b, pl.ds(ROUND_ROWS[r] * CHUNK, CHUNK), :]

    def h_send(b, r, to, sem):
        copy(h_ref(b, r), h_ref(b, r), send.at[sem], hsem.at[b * CHUNKS + r], to).start()

    def h_x(b, r, sides=(1, -1)):
        for side in sides:
            h_send(b, r, x_to[side], 3)

    def h_y(b, r, sides=(1, -1)):
        for side in sides:
            h_send(b, r, y_to[side], 4)

    def h_wait(b, r):
        copy(h_ref(b, r), h_ref(b, r), send.at[3], hsem.at[b * CHUNKS + r], sibling).wait_recv()

    own_block = block(x, y_hi, core)
    own_piece = piece_of(x, y, z)
    my_group = x * 4 + y

    def local_hidden(r):
        rows = pl.ds(ROUND_ROWS[r] * CHUNK, CHUNK)
        return pltpu.make_async_copy(hidden.at[rows, :], h_ref(own_block, r),
                                     hsem.at[own_block * CHUNKS + r])

    def local_weights(part):
        return pltpu.make_async_copy(
            weights.at[:, pl.ds(pl.multiple_of(part * D + my_group * WIDTH, WIDTH), WIDTH)],
            wbuf.at[part, rows_of(own_piece, core), :], misc.at[2 + part])

    for part in range(3):
        local_weights(part).start()

    @pl.when(across == 0)
    def _():
        for r in range(CHUNKS):
            local_hidden(r).start()

    barrier = pltpu.get_barrier_semaphore()
    greeted = [device(mx, my, z, core) for mx, my in mates_to[1:]]
    greeted += [z_to[1], z_to[-1], sibling, partner,
                device(x, y, above, 1 - core), device(x, y, below, 1 - core)]
    for to in greeted:
        pl.semaphore_signal(barrier, inc=1, device_id=to, device_id_type=MESH)
    pl.semaphore_wait(barrier, len(greeted))

    def all_to_all(i):
        mx, my = mates_to[i]
        for part in range(3):
            columns = pl.ds(pl.multiple_of(part * D + (mx * 4 + my) * WIDTH, WIDTH), WIDTH)
            copy(weights.at[:, columns], wbuf.at[part, rows_of(own_piece, core), :],
                 send.at[0], wsem.at[own_piece], device(mx, my, z, core)).start()

    @pl.when(across == 1)
    def _():
        for r in range(CHUNKS):
            rows = pl.ds(ROUND_ROWS[r] * CHUNK, CHUNK)
            copy(hidden.at[rows, :], h_ref(own_block, r), send.at[5],
                 hsem.at[own_block * CHUNKS + r], sibling).start()

    def own_weights(i):
        mx, my = mates[i]
        piece = piece_of(mx, my, z)
        if i == 0:
            for part in range(3):
                local_weights(part).wait()
        else:
            w_wait(piece)
        w_send(piece, z_to[1], 1)
        w_send(piece, z_to[-1], 1)
        w_sib(piece, ORDER[i][1] % 2)

    def near_weights(i):
        mx, my = mates[i]
        piece = piece_of(mx, my, below)
        w_wait(piece)
        if i % 2 == 0:
            w_send(piece, z_to[1], 1)
        w_sib(piece, 6 + ORDER[i][1] % 2)
        piece = piece_of(mx, my, above)
        w_wait(piece)
        if i % 2 == 1:
            w_send(piece, z_to[-1], 1)
        w_sib(piece, 2 + ORDER[i][1] % 2)

    def far_weights(i):
        mx, my = mates[i]
        piece = piece_of(mx, my, (z + 2) % 4)
        w_wait(piece)
        w_sib(piece, 4 + ORDER[i][1] % 2)

    yh_down, yh_up = down // 2, up // 2

    def hidden0(r):
        @pl.when(across == 0)
        def _():
            a, b = block(x, y_hi, 0), block(x, y_hi, 1)
            h_wait(a, r)
            h_x(a, r)
            h_wait(b, r)
            h_y(b, r)

    def hidden0b(r):
        @pl.when(across == 0)
        def _():
            h_y(block(x, y_hi, 0), r)
            h_x(block(x, y_hi, 1), r)

    def hidden1(r):
        @pl.when(across == 0)
        def _():
            a = block(left, y_hi, 0)
            h_wait(a, r)
            if r % 2 == 0:
                h_x(a, r, (1,))
            h_y(a, r)
            a = block(right, y_hi, 0)
            h_wait(a, r)
            if r % 2 == 1:
                h_x(a, r, (-1,))
            h_y(a, r)

        @pl.when(across == 1)
        def _():
            b = block(x, yh_down, 1)
            h_wait(b, r)
            if r % 2 == 0:
                h_y(b, r, (1,))
            h_x(b, r)
            b = block(x, yh_up, 1)
            h_wait(b, r)
            if r % 2 == 1:
                h_y(b, r, (-1,))
            h_x(b, r)

    def hidden2(r):
        @pl.when(across == 0)
        def _():
            a = block((x + 2) % 4, y_hi, 0)
            h_wait(a, r)
            h_y(a, r)
            b = block(x, 1 - y_hi, 1)
            h_wait(b, r)
            h_x(b, r)

    xs_steps = (x, left, right, (x + 2) % 4)

    def hidden3a(m, r):
        @pl.when(across == 1)
        def _():
            a = block(xs_steps[m], yh_down, 0)
            h_wait(a, r)
            if (m + r) % 2 == 0:
                h_y(a, r, (1,))
            a = block(xs_steps[m], yh_up, 0)
            h_wait(a, r)
            if (m + r) % 2 == 1:
                h_y(a, r, (-1,))

    def hidden3b(r):
        for yh in range(2):
            b = block(left, yh, 1)
            h_wait(b, r)
            if (yh + r) % 2 == 0:
                h_x(b, r, (1,))
            b = block(right, yh, 1)
            h_wait(b, r)
            if (yh + r) % 2 == 1:
                h_x(b, r, (-1,))

    def hidden4a(m, r):
        @pl.when(across == 0)
        def _():
            h_wait(block(xs_steps[m], 1 - y_hi, 0), r)

    def hidden4b(r):
        for yh in range(2):
            h_wait(block((x + 2) % 4, yh, 1), r)

    def make_taps():
        bank8[0:TAPS, :] = bank[...]
        bank8[TAPS:, :] = jnp.zeros((8 - TAPS, FILTERS), jnp.float32)

        @pl.when(across == 0)
        def _():
            filters = lax.broadcasted_iota(jnp.int32, (FILTERS, WIDTH), 0)
            selector = (filters == assigned[...]).astype(jnp.float32)
            taps[...] = jnp.dot(bank8[...], selector, precision=lax.Precision.HIGHEST,
                                preferred_element_type=jnp.float32)
            copy(taps, taps, send.at[6], misc.at[0], sibling).start()

        @pl.when(across == 1)
        def _():
            copy(taps, taps, send.at[6], misc.at[0], sibling).wait_recv()

        prod[0:8, :] = jnp.zeros((8, WIDTH), jnp.float32)

    codes = [(kind == "x") * 32 + r * 8 + step * 2 + half for kind, r, step, half in DOTS]
    words = [sum(code << 6 * i for i, code in enumerate(codes[first:first + 5]))
             for first in range(0, len(codes), 5)]

    def dot(s):
        word = jnp.int32(words[0])
        for i in range(1, len(words)):
            word = jnp.where(s >= 5 * i, jnp.int32(words[i]), word)
        code = lax.shift_right_logical(word, 6 * (s % 5)) % 64
        by_x, r, step, half = code // 32, code // 8 % 4, code // 2 % 4, code % 2
        z_block = ((y_lo + half) % 2) * 4 + (z + step) % 4
        shift = jnp.where(step == 0, 0, jnp.where(step == 1, 3, step - 1))
        x_block = ((x + shift) % 4) * 2 + half
        b = jnp.where(by_x == 1, x_block, z_block)
        rows = pl.ds(pl.multiple_of((r + 3) % 4 * CHUNK, CHUNK), CHUNK)
        depth = pl.ds(pl.multiple_of(b * 1024, 1024), 1024)
        left_side = jnp.concatenate([hbuf[2 * b, rows, :], hbuf[2 * b + 1, rows, :]], axis=1)
        for part in range(3):
            acc[rows, part * WIDTH:(part + 1) * WIDTH] += jnp.dot(
                left_side, wbuf[part, depth, :], preferred_element_type=jnp.float32)

    SUB = 32

    def products(base):
        def step(i, _):
            rows = pl.ds(pl.multiple_of(base + i * SUB, SUB), SUB)
            prod[pl.ds(pl.multiple_of(base + i * SUB + 8, 8), SUB), :] = (
                acc[rows, WIDTH:2 * WIDTH] * acc[rows, 2 * WIDTH:])
            return 0
        lax.fori_loop(0, CHUNK // SUB, step, 0)

    def filtered(base, count, size):
        def step(i, _):
            first = pl.multiple_of(base + i * size, size)
            near = prod[pl.ds(first, size + 8), :]
            total = jnp.zeros((size, WIDTH), jnp.float32)
            for j in range(TAPS):
                total = total + taps[j:j + 1, :] * near[8 - j:8 - j + size, :]
            rows = pl.ds(first, size)
            stage[rows, :] = (acc[rows, 0:WIDTH] * total).astype(jnp.bfloat16)
            return 0
        lax.fori_loop(0, count, step, 0)

    def out_send(first, count, sem):
        src, dst = stage.at[pl.ds(first, count), :], out.at[pl.ds(first, count), :]

        @pl.when(across == 0)
        def _():
            pltpu.make_async_copy(src, dst, misc.at[sem]).start()

        @pl.when(across == 1)
        def _():
            copy(src, dst, send.at[8], misc.at[sem], partner).start()

    def out_wait(first, count, sem):
        src, dst = stage.at[pl.ds(first, count), :], out.at[pl.ds(first, count), :]

        @pl.when(across == 0)
        def _():
            pltpu.make_async_copy(src, dst, misc.at[sem]).wait()

        @pl.when(across == 1)
        def _():
            copy(src, dst, send.at[8], misc.at[sem], partner).wait_recv()

    halo_from, halo_to = prod.at[pl.ds(TOKENS, 8), :], prod.at[pl.ds(0, 8), :]
    last_window = (z == 3) & (core == 1)
    first_window = (z == 0) & (core == 0)
    next_core = jnp.where(z == 3, 1 - core, core)

    def halo():
        return copy(halo_from, halo_to, send.at[7], misc.at[1], device(x, y, above, next_core))

    def epilogue0():
        products(3 * CHUNK)

        @pl.when(jnp.logical_not(last_window))
        def _():
            halo().start()

        filtered(3 * CHUNK + 32, 7, 32)
        out_send(3 * CHUNK + 32, CHUNK - 32, 5)

    def epilogue1():
        products(0)

        @pl.when(jnp.logical_not(first_window))
        def _():
            halo().wait_recv()

        filtered(0, 8, 32)
        out_send(0, CHUNK, 6)

    def epilogue2():
        products(CHUNK)
        filtered(CHUNK, 8, 32)
        out_send(CHUNK, CHUNK, 7)

    def epilogue3():
        products(2 * CHUNK)
        filtered(2 * CHUNK, 9, 32)
        out_send(2 * CHUNK, CHUNK + 32, 8)

    def zero_acc():
        def step(i, _):
            rows = pl.ds(pl.multiple_of(i * 32, 32), 32)
            acc[rows, :] = jnp.zeros((32, 3 * WIDTH), jnp.float32)
            return 0
        lax.fori_loop(0, TOKENS // 32, step, 0)

    run = {"taps": make_taps, "zero": zero_acc, "all": all_to_all, "own": own_weights, "near": near_weights, "far": far_weights, "sib": sib_wait,
           "h0": hidden0, "h0b": hidden0b, "h1": hidden1, "h2": hidden2, "h3a": hidden3a, "h3b": hidden3b,
           "h4a": hidden4a, "h4b": hidden4b}
    before = timeline()
    last_dot = {r: max(s for s in range(len(DOTS)) if DOTS[s][1] == r) for r in range(CHUNKS)}

    def slot_step(s, _):
        for k in range(len(DOTS)):
            @pl.when(s == k)
            def _(k=k):
                for name, *args in before[k]:
                    run[name](*args)
                for r, epilogue in enumerate((epilogue0, epilogue1, epilogue2)):
                    if k == max(last_dot[i] for i in range(r + 1)) + 1:
                        epilogue()
        dot(s)
        return 0
    lax.fori_loop(0, len(DOTS), slot_step, 0)
    epilogue3()

    out_wait(3 * CHUNK + 32, CHUNK - 32, 5)
    out_wait(0, CHUNK, 6)
    out_wait(CHUNK, CHUNK, 7)
    out_wait(2 * CHUNK, CHUNK + 32, 8)

    def sent(ref, sem):
        copy(ref, ref, send.at[sem], misc.at[0], sibling).wait_send()

    sent(wbuf.at[:, pl.ds(0, 15 * ROWS), :], 0)
    sent(wbuf.at[:, pl.ds(0, 48 * ROWS), :], 1)
    sent(wbuf.at[:, pl.ds(0, 64 * ROWS), :], 2)

    @pl.when(across == 0)
    def _():
        sent(hbuf.at[pl.ds(0, 9)], 3)
        sent(hbuf.at[pl.ds(0, 10)], 4)
        sent(taps, 6)

    @pl.when(across == 1)
    def _():
        sent(hbuf.at[pl.ds(0, 6)], 3)
        sent(hbuf.at[pl.ds(0, 5)], 4)
        sent(hidden, 5)
        sent(stage, 8)

    @pl.when(jnp.logical_not(last_window))
    def _():
        halo().wait_send()


def on_device(hidden, in_weights, filter_bank, assignment):
    assigned = jnp.repeat(assignment, GROUP)[None, :]
    any_space = pl.BlockSpec(memory_space=pl.ANY)
    vmem = pl.BlockSpec(memory_space=pltpu.VMEM)
    return pl.pallas_call(
        kernel,
        name="hyena",
        out_shape=jax.ShapeDtypeStruct((TOKENS, WIDTH), jnp.bfloat16),
        in_specs=[any_space, any_space, vmem, vmem],
        out_specs=any_space,
        scratch_shapes=[
            pltpu.VMEM((16, TOKENS, WIDTH), jnp.bfloat16),
            pltpu.VMEM((3, D, WIDTH), jnp.bfloat16),
            pltpu.VMEM((TOKENS, 3 * WIDTH), jnp.float32),
            pltpu.VMEM((TOKENS + 8, WIDTH), jnp.float32),
            pltpu.VMEM((TOKENS, WIDTH), jnp.bfloat16),
            pltpu.VMEM((8, WIDTH), jnp.float32),
            pltpu.VMEM((8, FILTERS), jnp.float32),
            pltpu.SemaphoreType.DMA((16 * CHUNKS,)),
            pltpu.SemaphoreType.DMA((64,)),
            pltpu.SemaphoreType.DMA((8,)),
            pltpu.SemaphoreType.DMA((9,)),
            pltpu.SemaphoreType.DMA((9,)),
        ],
        compiler_params=pltpu.CompilerParams(
            collective_id=0, has_side_effects=True, vmem_limit_bytes=60 * 2**20),
        cost_estimate=pl.CostEstimate(
            flops=2 * TOKENS * D * 3 * WIDTH, bytes_accessed=44 * 2**20, transcendentals=0),
    )(hidden, in_weights, filter_bank, assigned)


def solution(mesh):
    in_specs = (P("seq", "chan"), P(("seq", "chan"), None), P(), P("chan"))
    return jax.shard_map(
        on_device, mesh=mesh, in_specs=in_specs, out_specs=P("seq", "chan"), check_vma=False)
```

```python
import jax
import jax.numpy as jnp
from jax import lax
from jax.experimental import pallas as pl
from jax.experimental.pallas import tpu as pltpu
from jax.sharding import PartitionSpec as P

D = 8192
GROUP = 16
TAPS = 7
FILTERS = 512
TOKENS = 1024
WIDTH = 512
ROWS = 64
CHUNK = 256
CHUNKS = TOKENS // CHUNK
MESH = pl.DeviceIdType.MESH

ROUND_ROWS = (3, 0, 1, 2)
ORDER = ((0, 0), (1, 0), (3, 0), (0, 2), (2, 0), (1, 2), (3, 2), (2, 2),
         (0, 1), (0, 3), (1, 1), (3, 3), (1, 3), (3, 1), (2, 1), (2, 3))
FIRST, AFTER = 19.54, 20.63
STAGES = (0.0, 6.54, 23.09, 34.44, 49.63)
LAST = (12.84, 25.44, 35.22, 44.3, 71.25)
SPREAD = (2.51, 2.56)
SPLIT = 21.05
ALL = (0, 0.5)
OWN = (3.64, 1.48)
NEAR = (19.06, 1.08, 5.8)
FAR = (73.66, 4.68)
DOT = 1.7

HOPS = (0, 1, 3, 2)
DOTS = (
    ("z", 0, 0, 0), ("z", 0, 1, 0), ("z", 0, 3, 0), ("z", 1, 0, 0),
    ("z", 1, 1, 0), ("z", 1, 3, 0), ("z", 0, 0, 1), ("z", 0, 1, 1),
    ("z", 0, 3, 1), ("z", 1, 0, 1), ("z", 1, 1, 1), ("z", 1, 3, 1),
    ("z", 0, 2, 0), ("z", 1, 2, 0), ("z", 2, 0, 0), ("z", 2, 0, 1),
    ("z", 2, 1, 0), ("z", 2, 1, 1), ("z", 2, 3, 0), ("z", 2, 3, 1),
    ("z", 2, 2, 0), ("z", 0, 2, 1), ("z", 1, 2, 1), ("z", 2, 2, 1),
    ("x", 3, 0, 0), ("x", 3, 0, 1), ("x", 3, 1, 0), ("x", 3, 1, 1),
    ("x", 3, 2, 0), ("x", 3, 2, 1), ("x", 3, 3, 0), ("x", 3, 3, 1),
)


def hidden_needs(m, r):
    return [("h3a", m, r), ("h4a", m, r)] + [
        [("h1", r), ("h2", r)], [("h1", r), ("h3b", r)], [("h1", r), ("h3b", r)],
        [("h2", r), ("h4b", r)]][m]


def timeline():
    when = {("taps",): 30.0, ("zero",): 33.0}
    for i in range(16):
        if i:
            when["all", i] = ALL[0] + ALL[1] * i
        when["own", i] = OWN[0] + OWN[1] * i
        when["near", i] = max(NEAR[0], NEAR[1] + NEAR[2] * i)
        when["far", i] = FAR[0] + FAR[1] * (i // 2 + 1)
    for r in range(CHUNKS):
        start = FIRST + AFTER * r
        stages = STAGES if r < CHUNKS - 1 else LAST
        when["h0b", r] = start + stages[0] + SPLIT
        for index in range(3):
            when["h%d" % index, r] = start + stages[index]
        for m in range(4):
            when["h3a", m, r] = start + stages[3] + SPREAD[0] * m
            when["h4a", m, r] = start + stages[4] + SPREAD[1] * m
        when["h3b", r] = start + stages[3] + SPREAD[0] * 1.5
        when["h4b", r] = start + stages[4] + SPREAD[1] * 2.5
    kinds = {0: "own", 1: "near", 3: "near", 2: "far"}
    for hop in HOPS:
        for half in range(2):
            last = max(when[kinds[hop], i] for i in range(16) if ORDER[i][1] % 2 == half)
            when["sib", hop, half] = last + 3.0

    slots, placed, clock = [], set(), 0.0
    names = list(when)
    for kind, r, step, half in DOTS:
        if kind == "z":
            needs = [key for m in range(4) for key in hidden_needs(m, r)] + [("sib", step, half)]
        else:
            needs = hidden_needs(step, r) + [("sib", hop, h) for hop in HOPS for h in range(2)]
        clock = max([clock + DOT] + [when[key] for key in needs])
        ready = [key for key in names if when[key] <= clock and key not in placed]
        ready = sorted(ready, key=when.get)
        placed.update(ready)
        slots.append(ready)
    rest = [key for key in names if key not in placed]
    assert not rest
    return slots


def device(x, y, z, core):
    return ((y % 2) * 4 + z, x * 4 + (y // 2) * 2 + core)


def kernel(hidden, weights, bank, assigned, out, hbuf, wbuf, acc, prod, stage, taps, bank8,
           hsem, wsem, sibsem, misc, send):
    seq, chan = lax.axis_index("seq"), lax.axis_index("chan")
    x, y, z, core = chan // 4, (chan // 2 % 2) * 2 + seq // 4, seq % 4, chan % 2
    y_hi, y_lo = y // 2, y % 2
    across = (y_lo + core) % 2
    left, right = (x + 3) % 4, (x + 1) % 4
    down, up = (y + 3) % 4, (y + 1) % 4
    below, above = (z + 3) % 4, (z + 1) % 4
    sibling = device(x, y, z, 1 - core)
    partner = device(x, y + 1 - 2 * y_lo, z, 1 - core)
    x_to = {1: device(right, y, z, core), -1: device(left, y, z, core)}
    y_to = {1: device(x, up, z, core), -1: device(x, down, z, core)}
    z_to = {1: device(x, y, above, core), -1: device(x, y, below, core)}

    sign = 1 - 2 * core
    mates_to = [((x + sign * dx + 4) % 4, (y + sign * dy + 4) % 4) for dx, dy in ORDER]
    mates = [((x - sign * dx + 4) % 4, (y - sign * dy + 4) % 4) for dx, dy in ORDER]

    def copy(src, dst, send_sem, recv_sem, to):
        return pltpu.make_async_remote_copy(
            src_ref=src, dst_ref=dst, send_sem=send_sem, recv_sem=recv_sem,
            device_id=to, device_id_type=MESH)

    def rows_of(piece, owner):
        return pl.ds(pl.multiple_of((piece * 2 + owner) * ROWS, ROWS), ROWS)

    def piece_of(xs, ys, zs):
        return ((ys % 2) * 4 + zs) * 8 + xs * 2 + ys // 2

    def w_send(piece, to, sem):
        ref = wbuf.at[:, rows_of(piece, core), :]
        copy(ref, ref, send.at[sem], wsem.at[piece], to).start()

    def w_sib(piece, group):
        ref = wbuf.at[:, rows_of(piece, core), :]
        copy(ref, ref, send.at[2], sibsem.at[group], sibling).start()

    def w_wait(piece):
        ref = wbuf.at[:, rows_of(piece, core), :]
        copy(ref, ref, send.at[0], wsem.at[piece], sibling).wait_recv()

    def sib_wait(hop, half):
        ref = wbuf.at[:, pl.ds(0, 8 * ROWS), :]
        copy(ref, ref, send.at[2], sibsem.at[2 * hop + half], sibling).wait_recv()

    def block(xs, yh, ks):
        return xs * 4 + yh * 2 + ks

    def h_ref(b, r):
        return hbuf.at[b, pl.ds(ROUND_ROWS[r] * CHUNK, CHUNK), :]

    def h_send(b, r, to, sem):
        copy(h_ref(b, r), h_ref(b, r), send.at[sem], hsem.at[b * CHUNKS + r], to).start()

    def h_x(b, r, sides=(1, -1)):
        for side in sides:
            h_send(b, r, x_to[side], 3)

    def h_y(b, r, sides=(1, -1)):
        for side in sides:
            h_send(b, r, y_to[side], 4)

    def h_wait(b, r):
        copy(h_ref(b, r), h_ref(b, r), send.at[3], hsem.at[b * CHUNKS + r], sibling).wait_recv()

    own_block = block(x, y_hi, core)
    own_piece = piece_of(x, y, z)
    my_group = x * 4 + y

    def local_hidden(r):
        rows = pl.ds(ROUND_ROWS[r] * CHUNK, CHUNK)
        return pltpu.make_async_copy(hidden.at[rows, :], h_ref(own_block, r),
                                     hsem.at[own_block * CHUNKS + r])

    def local_weights(part):
        return pltpu.make_async_copy(
            weights.at[:, pl.ds(pl.multiple_of(part * D + my_group * WIDTH, WIDTH), WIDTH)],
            wbuf.at[part, rows_of(own_piece, core), :], misc.at[2 + part])

    for part in range(3):
        local_weights(part).start()

    @pl.when(across == 0)
    def _():
        for r in range(CHUNKS):
            local_hidden(r).start()

    barrier = pltpu.get_barrier_semaphore()
    greeted = [device(mx, my, z, core) for mx, my in mates_to[1:]]
    greeted += [z_to[1], z_to[-1], sibling, partner,
                device(x, y, above, 1 - core), device(x, y, below, 1 - core)]
    for to in greeted:
        pl.semaphore_signal(barrier, inc=1, device_id=to, device_id_type=MESH)
    pl.semaphore_wait(barrier, len(greeted))

    def all_to_all(i):
        mx, my = mates_to[i]
        for part in range(3):
            columns = pl.ds(pl.multiple_of(part * D + (mx * 4 + my) * WIDTH, WIDTH), WIDTH)
            copy(weights.at[:, columns], wbuf.at[part, rows_of(own_piece, core), :],
                 send.at[0], wsem.at[own_piece], device(mx, my, z, core)).start()

    @pl.when(across == 1)
    def _():
        for r in range(CHUNKS):
            rows = pl.ds(ROUND_ROWS[r] * CHUNK, CHUNK)
            copy(hidden.at[rows, :], h_ref(own_block, r), send.at[5],
                 hsem.at[own_block * CHUNKS + r], sibling).start()

    def own_weights(i):
        mx, my = mates[i]
        piece = piece_of(mx, my, z)
        if i == 0:
            for part in range(3):
                local_weights(part).wait()
        else:
            w_wait(piece)
        w_send(piece, z_to[1], 1)
        w_send(piece, z_to[-1], 1)
        w_sib(piece, ORDER[i][1] % 2)

    def near_weights(i):
        mx, my = mates[i]
        piece = piece_of(mx, my, below)
        w_wait(piece)
        if i % 2 == 0:
            w_send(piece, z_to[1], 1)
        w_sib(piece, 6 + ORDER[i][1] % 2)
        piece = piece_of(mx, my, above)
        w_wait(piece)
        if i % 2 == 1:
            w_send(piece, z_to[-1], 1)
        w_sib(piece, 2 + ORDER[i][1] % 2)

    def far_weights(i):
        mx, my = mates[i]
        piece = piece_of(mx, my, (z + 2) % 4)
        w_wait(piece)
        w_sib(piece, 4 + ORDER[i][1] % 2)

    yh_down, yh_up = down // 2, up // 2

    def hidden0(r):
        @pl.when(across == 0)
        def _():
            a, b = block(x, y_hi, 0), block(x, y_hi, 1)
            h_wait(a, r)
            h_x(a, r)
            h_wait(b, r)
            h_y(b, r)

    def hidden0b(r):
        @pl.when(across == 0)
        def _():
            h_y(block(x, y_hi, 0), r)
            h_x(block(x, y_hi, 1), r)

    def hidden1(r):
        @pl.when(across == 0)
        def _():
            a = block(left, y_hi, 0)
            h_wait(a, r)
            if r % 2 == 0:
                h_x(a, r, (1,))
            h_y(a, r)
            a = block(right, y_hi, 0)
            h_wait(a, r)
            if r % 2 == 1:
                h_x(a, r, (-1,))
            h_y(a, r)

        @pl.when(across == 1)
        def _():
            b = block(x, yh_down, 1)
            h_wait(b, r)
            if r % 2 == 0:
                h_y(b, r, (1,))
            h_x(b, r)
            b = block(x, yh_up, 1)
            h_wait(b, r)
            if r % 2 == 1:
                h_y(b, r, (-1,))
            h_x(b, r)

    def hidden2(r):
        @pl.when(across == 0)
        def _():
            a = block((x + 2) % 4, y_hi, 0)
            h_wait(a, r)
            h_y(a, r)
            b = block(x, 1 - y_hi, 1)
            h_wait(b, r)
            h_x(b, r)

    xs_steps = (x, left, right, (x + 2) % 4)

    def hidden3a(m, r):
        @pl.when(across == 1)
        def _():
            a = block(xs_steps[m], yh_down, 0)
            h_wait(a, r)
            if (m + r) % 2 == 0:
                h_y(a, r, (1,))
            a = block(xs_steps[m], yh_up, 0)
            h_wait(a, r)
            if (m + r) % 2 == 1:
                h_y(a, r, (-1,))

    def hidden3b(r):
        for yh in range(2):
            b = block(left, yh, 1)
            h_wait(b, r)
            if (yh + r) % 2 == 0:
                h_x(b, r, (1,))
            b = block(right, yh, 1)
            h_wait(b, r)
            if (yh + r) % 2 == 1:
                h_x(b, r, (-1,))

    def hidden4a(m, r):
        @pl.when(across == 0)
        def _():
            h_wait(block(xs_steps[m], 1 - y_hi, 0), r)

    def hidden4b(r):
        for yh in range(2):
            h_wait(block((x + 2) % 4, yh, 1), r)

    def make_taps():
        bank8[0:TAPS, :] = bank[...]
        bank8[TAPS:, :] = jnp.zeros((8 - TAPS, FILTERS), jnp.float32)

        @pl.when(across == 0)
        def _():
            filters = lax.broadcasted_iota(jnp.int32, (FILTERS, WIDTH), 0)
            selector = (filters == assigned[...]).astype(jnp.float32)
            taps[...] = jnp.dot(bank8[...], selector, precision=lax.Precision.HIGHEST,
                                preferred_element_type=jnp.float32)
            copy(taps, taps, send.at[6], misc.at[0], sibling).start()

        @pl.when(across == 1)
        def _():
            copy(taps, taps, send.at[6], misc.at[0], sibling).wait_recv()

        prod[0:8, :] = jnp.zeros((8, WIDTH), jnp.float32)

    codes = [(kind == "x") * 32 + r * 8 + step * 2 + half for kind, r, step, half in DOTS]
    words = [sum(code << 6 * i for i, code in enumerate(codes[first:first + 5]))
             for first in range(0, len(codes), 5)]

    def dot(s):
        word = jnp.int32(words[0])
        for i in range(1, len(words)):
            word = jnp.where(s >= 5 * i, jnp.int32(words[i]), word)
        code = lax.shift_right_logical(word, 6 * (s % 5)) % 64
        by_x, r, step, half = code // 32, code // 8 % 4, code // 2 % 4, code % 2
        z_block = ((y_lo + half) % 2) * 4 + (z + step) % 4
        shift = jnp.where(step == 0, 0, jnp.where(step == 1, 3, step - 1))
        x_block = ((x + shift) % 4) * 2 + half
        b = jnp.where(by_x == 1, x_block, z_block)
        rows = pl.ds(pl.multiple_of((r + 3) % 4 * CHUNK, CHUNK), CHUNK)
        depth = pl.ds(pl.multiple_of(b * 1024, 1024), 1024)
        left_side = jnp.concatenate([hbuf[2 * b, rows, :], hbuf[2 * b + 1, rows, :]], axis=1)
        for part in range(3):
            acc[rows, part * WIDTH:(part + 1) * WIDTH] += jnp.dot(
                left_side, wbuf[part, depth, :], preferred_element_type=jnp.float32)

    SUB = 32

    def products(base):
        def step(i, _):
            rows = pl.ds(pl.multiple_of(base + i * SUB, SUB), SUB)
            prod[pl.ds(pl.multiple_of(base + i * SUB + 8, 8), SUB), :] = (
                acc[rows, WIDTH:2 * WIDTH] * acc[rows, 2 * WIDTH:])
            return 0
        lax.fori_loop(0, CHUNK // SUB, step, 0)

    def filtered(base, count, size):
        def step(i, _):
            first = pl.multiple_of(base + i * size, size)
            near = prod[pl.ds(first, size + 8), :]
            total = jnp.zeros((size, WIDTH), jnp.float32)
            for j in range(TAPS):
                total = total + taps[j:j + 1, :] * near[8 - j:8 - j + size, :]
            rows = pl.ds(first, size)
            stage[rows, :] = (acc[rows, 0:WIDTH] * total).astype(jnp.bfloat16)
            return 0
        lax.fori_loop(0, count, step, 0)

    def out_send(first, count, sem):
        src, dst = stage.at[pl.ds(first, count), :], out.at[pl.ds(first, count), :]

        @pl.when(across == 0)
        def _():
            pltpu.make_async_copy(src, dst, misc.at[sem]).start()

        @pl.when(across == 1)
        def _():
            copy(src, dst, send.at[8], misc.at[sem], partner).start()

    def out_wait(first, count, sem):
        src, dst = stage.at[pl.ds(first, count), :], out.at[pl.ds(first, count), :]

        @pl.when(across == 0)
        def _():
            pltpu.make_async_copy(src, dst, misc.at[sem]).wait()

        @pl.when(across == 1)
        def _():
            copy(src, dst, send.at[8], misc.at[sem], partner).wait_recv()

    halo_from, halo_to = prod.at[pl.ds(TOKENS, 8), :], prod.at[pl.ds(0, 8), :]
    last_window = (z == 3) & (core == 1)
    first_window = (z == 0) & (core == 0)
    next_core = jnp.where(z == 3, 1 - core, core)

    def halo():
        return copy(halo_from, halo_to, send.at[7], misc.at[1], device(x, y, above, next_core))

    def epilogue0():
        products(3 * CHUNK)

        @pl.when(jnp.logical_not(last_window))
        def _():
            halo().start()

        filtered(3 * CHUNK + 32, 7, 32)
        out_send(3 * CHUNK + 32, CHUNK - 32, 5)

    def epilogue1():
        products(0)

        @pl.when(jnp.logical_not(first_window))
        def _():
            halo().wait_recv()

        filtered(0, 8, 32)
        out_send(0, CHUNK, 6)

    def epilogue2():
        products(CHUNK)
        filtered(CHUNK, 8, 32)
        out_send(CHUNK, CHUNK, 7)

    def epilogue3():
        products(2 * CHUNK)
        filtered(2 * CHUNK, 9, 32)
        out_send(2 * CHUNK, CHUNK + 32, 8)

    def zero_acc():
        def step(i, _):
            rows = pl.ds(pl.multiple_of(i * 32, 32), 32)
            acc[rows, :] = jnp.zeros((32, 3 * WIDTH), jnp.float32)
            return 0
        lax.fori_loop(0, TOKENS // 32, step, 0)

    run = {"taps": make_taps, "zero": zero_acc, "all": all_to_all, "own": own_weights, "near": near_weights, "far": far_weights, "sib": sib_wait,
           "h0": hidden0, "h0b": hidden0b, "h1": hidden1, "h2": hidden2, "h3a": hidden3a, "h3b": hidden3b,
           "h4a": hidden4a, "h4b": hidden4b}
    before = timeline()
    last_dot = {r: max(s for s in range(len(DOTS)) if DOTS[s][1] == r) for r in range(CHUNKS)}

    def slot_step(s, _):
        for k in range(len(DOTS)):
            @pl.when(s == k)
            def _(k=k):
                for name, *args in before[k]:
                    run[name](*args)
                for r, epilogue in enumerate((epilogue0, epilogue1, epilogue2)):
                    if k == max(last_dot[i] for i in range(r + 1)) + 1:
                        epilogue()
        dot(s)
        return 0
    lax.fori_loop(0, len(DOTS), slot_step, 0)
    epilogue3()

    out_wait(3 * CHUNK + 32, CHUNK - 32, 5)
    out_wait(0, CHUNK, 6)
    out_wait(CHUNK, CHUNK, 7)
    out_wait(2 * CHUNK, CHUNK + 32, 8)

    def sent(ref, sem):
        copy(ref, ref, send.at[sem], misc.at[0], sibling).wait_send()

    sent(wbuf.at[:, pl.ds(0, 15 * ROWS), :], 0)
    sent(wbuf.at[:, pl.ds(0, 48 * ROWS), :], 1)
    sent(wbuf.at[:, pl.ds(0, 64 * ROWS), :], 2)

    @pl.when(across == 0)
    def _():
        sent(hbuf.at[pl.ds(0, 9)], 3)
        sent(hbuf.at[pl.ds(0, 10)], 4)
        sent(taps, 6)

    @pl.when(across == 1)
    def _():
        sent(hbuf.at[pl.ds(0, 6)], 3)
        sent(hbuf.at[pl.ds(0, 5)], 4)
        sent(hidden, 5)
        sent(stage, 8)

    @pl.when(jnp.logical_not(last_window))
    def _():
        halo().wait_send()


def on_device(hidden, in_weights, filter_bank, assignment):
    assigned = jnp.repeat(assignment, GROUP)[None, :]
    any_space = pl.BlockSpec(memory_space=pl.ANY)
    vmem = pl.BlockSpec(memory_space=pltpu.VMEM)
    return pl.pallas_call(
        kernel,
        name="hyena",
        out_shape=jax.ShapeDtypeStruct((TOKENS, WIDTH), jnp.bfloat16),
        in_specs=[any_space, any_space, vmem, vmem],
        out_specs=any_space,
        scratch_shapes=[
            pltpu.VMEM((16, TOKENS, WIDTH), jnp.bfloat16),
            pltpu.VMEM((3, D, WIDTH), jnp.bfloat16),
            pltpu.VMEM((TOKENS, 3 * WIDTH), jnp.float32),
            pltpu.VMEM((TOKENS + 8, WIDTH), jnp.float32),
            pltpu.VMEM((TOKENS, WIDTH), jnp.bfloat16),
            pltpu.VMEM((8, WIDTH), jnp.float32),
            pltpu.VMEM((8, FILTERS), jnp.float32),
            pltpu.SemaphoreType.DMA((16 * CHUNKS,)),
            pltpu.SemaphoreType.DMA((64,)),
            pltpu.SemaphoreType.DMA((8,)),
            pltpu.SemaphoreType.DMA((9,)),
            pltpu.SemaphoreType.DMA((9,)),
        ],
        compiler_params=pltpu.CompilerParams(
            collective_id=0, has_side_effects=True, vmem_limit_bytes=60 * 2**20),
        cost_estimate=pl.CostEstimate(
            flops=2 * TOKENS * D * 3 * WIDTH, bytes_accessed=44 * 2**20, transcendentals=0),
    )(hidden, in_weights, filter_bank, assigned)


def solution(mesh):
    in_specs = (P("seq", "chan"), P(("seq", "chan"), None), P(), P("chan"))
    return jax.shard_map(
        on_device, mesh=mesh, in_specs=in_specs, out_specs=P("seq", "chan"), check_vma=False)
```

```python
import jax
import jax.numpy as jnp
from jax import lax
from jax.experimental import pallas as pl
from jax.experimental.pallas import tpu as pltpu
from jax.sharding import PartitionSpec as P

D = 8192
GROUP = 16
TAPS = 7
FILTERS = 512
TOKENS = 1024
WIDTH = 512
ROWS = 64
CHUNK = 256
CHUNKS = TOKENS // CHUNK
MESH = pl.DeviceIdType.MESH

ROUNDS = ((768, 256), (0, 256), (256, 256), (512, 256))
ORDER = ((0, 0), (1, 0), (3, 0), (0, 2), (2, 0), (1, 2), (3, 2), (2, 2),
         (0, 1), (0, 3), (1, 1), (3, 3), (1, 3), (3, 1), (2, 1), (2, 3))
STARTS = (19.54, 40.17, 60.8, 81.43)
STAGES = (0.0, 6.54, 23.09, 34.44, 49.63)
LAST = (12.84, 25.44, 35.22, 44.3, 71.25)
SPREAD = (2.51, 2.56)
SPLIT = 21.05
ALL = (0, 0.5)
OWN = (3.64, 1.48)
NEAR = (19.06, 1.08, 5.8)
FAR = (73.66, 4.68)
DOT = 1.7

HOPS = (0, 1, 3, 2)
DOTS = (
    ("z", 0, 0, 0), ("z", 0, 1, 0), ("z", 0, 3, 0), ("z", 1, 0, 0),
    ("z", 1, 1, 0), ("z", 1, 3, 0), ("z", 0, 0, 1), ("z", 0, 1, 1),
    ("z", 0, 3, 1), ("z", 1, 0, 1), ("z", 1, 1, 1), ("z", 1, 3, 1),
    ("z", 0, 2, 0), ("z", 1, 2, 0), ("z", 2, 0, 0), ("z", 2, 0, 1),
    ("z", 2, 1, 0), ("z", 2, 1, 1), ("z", 2, 3, 0), ("z", 2, 3, 1),
    ("z", 2, 2, 0), ("z", 0, 2, 1), ("z", 1, 2, 1), ("z", 2, 2, 1),
    ("x", 3, 0, 1), ("x", 3, 0, 0), ("x", 3, 1, 0), ("x", 3, 1, 1),
    ("x", 3, 2, 0), ("x", 3, 2, 1), ("x", 3, 3, 0), ("x", 3, 3, 1),
)


def hidden_needs(m, r):
    return [("h3a", m, r), ("h4a", m, r)] + [
        [("h1", r), ("h2", r)], [("h1", r), ("h3b", r)], [("h1", r), ("h3b", r)],
        [("h2", r), ("h4b", r)]][m]


def timeline():
    when = {("taps",): 30.0, ("zero",): 33.0}
    for i in range(16):
        if i:
            when["all", i] = ALL[0] + ALL[1] * i
        when["own", i] = OWN[0] + OWN[1] * i
        when["near", i] = max(NEAR[0], NEAR[1] + NEAR[2] * i)
        when["far", i] = FAR[0] + FAR[1] * (i // 2 + 1)
    for r, start in enumerate(STARTS):
        stages = LAST if r == CHUNKS - 1 else STAGES
        when["h0b", r] = start + stages[0] + SPLIT
        for index in range(3):
            when["h%d" % index, r] = start + stages[index]
        for m in range(4):
            when["h3a", m, r] = start + stages[3] + SPREAD[0] * m
            when["h4a", m, r] = start + stages[4] + SPREAD[1] * m
        when["h3b", r] = start + stages[3] + SPREAD[0] * 1.5
        when["h4b", r] = start + stages[4] + SPREAD[1] * 2.5
    kinds = {0: "own", 1: "near", 3: "near", 2: "far"}
    for hop in HOPS:
        for half in range(2):
            last = max(when[kinds[hop], i] for i in range(16) if ORDER[i][1] % 2 == half)
            when["sib", hop, half] = last + 3.0

    slots, placed, clock = [], set(), 0.0
    names = list(when)
    for kind, r, step, half in DOTS:
        if kind == "z":
            needs = [key for m in range(4) for key in hidden_needs(m, r)]
            needs += [("sib", step, half)]
        else:
            needs = hidden_needs(step, r) + [
                ("sib", hop, h) for hop in HOPS for h in range(2)]
        clock = max([clock + DOT] + [when[key] for key in needs])
        ready = [key for key in names if when[key] <= clock and key not in placed]
        ready = sorted(ready, key=when.get)
        placed.update(ready)
        slots.append(ready)
    rest = [key for key in names if key not in placed]
    assert not rest
    return slots


def device(x, y, z, core):
    return ((y % 2) * 4 + z, x * 4 + (y // 2) * 2 + core)


def kernel(hidden, weights, bank, assigned, out, hbuf, wbuf, acc, prod, stage, taps, bank8,
           hsem, wsem, sibsem, misc, send):
    seq, chan = lax.axis_index("seq"), lax.axis_index("chan")
    x, y, z, core = chan // 4, (chan // 2 % 2) * 2 + seq // 4, seq % 4, chan % 2
    y_hi, y_lo = y // 2, y % 2
    across = (y_lo + core) % 2
    left, right = (x + 3) % 4, (x + 1) % 4
    down, up = (y + 3) % 4, (y + 1) % 4
    below, above = (z + 3) % 4, (z + 1) % 4
    sibling = device(x, y, z, 1 - core)
    partner = device(x, y + 1 - 2 * y_lo, z, 1 - core)
    x_to = {1: device(right, y, z, core), -1: device(left, y, z, core)}
    y_to = {1: device(x, up, z, core), -1: device(x, down, z, core)}
    z_to = {1: device(x, y, above, core), -1: device(x, y, below, core)}

    sign = 1 - 2 * core
    mates_to = [((x + sign * dx + 4) % 4, (y + sign * dy + 4) % 4) for dx, dy in ORDER]
    mates = [((x - sign * dx + 4) % 4, (y - sign * dy + 4) % 4) for dx, dy in ORDER]

    def copy(src, dst, send_sem, recv_sem, to):
        return pltpu.make_async_remote_copy(
            src_ref=src, dst_ref=dst, send_sem=send_sem, recv_sem=recv_sem,
            device_id=to, device_id_type=MESH)

    def rows_of(piece, owner):
        return pl.ds(pl.multiple_of((piece * 2 + owner) * ROWS, ROWS), ROWS)

    def piece_of(xs, ys, zs):
        return ((ys % 2) * 4 + zs) * 8 + xs * 2 + ys // 2

    def w_send(piece, to, sem):
        ref = wbuf.at[:, rows_of(piece, core), :]
        copy(ref, ref, send.at[sem], wsem.at[piece], to).start()

    def w_sib(piece, group):
        ref = wbuf.at[:, rows_of(piece, core), :]
        copy(ref, ref, send.at[2], sibsem.at[group], sibling).start()

    def w_wait(piece):
        ref = wbuf.at[:, rows_of(piece, core), :]
        copy(ref, ref, send.at[0], wsem.at[piece], sibling).wait_recv()

    def sib_wait(hop, half):
        ref = wbuf.at[:, pl.ds(0, 8 * ROWS), :]
        copy(ref, ref, send.at[2], sibsem.at[2 * hop + half], sibling).wait_recv()

    def block(xs, yh, ks):
        return xs * 4 + yh * 2 + ks

    def h_ref(b, r):
        return hbuf.at[b, pl.ds(*ROUNDS[r]), :]

    def h_sem(b, r):
        return hsem.at[b * len(ROUNDS) + r]

    def h_send(b, r, to, sem):
        copy(h_ref(b, r), h_ref(b, r), send.at[sem], h_sem(b, r), to).start()

    def h_x(b, r):
        for side in (1, -1):
            h_send(b, r, x_to[side], 3)

    def h_y(b, r):
        for side in (1, -1):
            h_send(b, r, y_to[side], 4)

    def pass_on(to, sem, side, b, r):
        h_send(b, r, to[side], sem)

    def h_wait(b, r):
        copy(h_ref(b, r), h_ref(b, r), send.at[3], h_sem(b, r), sibling).wait_recv()

    own_block = block(x, y_hi, core)
    own_piece = piece_of(x, y, z)
    my_group = x * 4 + y

    def local_hidden(r):
        rows = pl.ds(*ROUNDS[r])
        return pltpu.make_async_copy(hidden.at[rows, :], h_ref(own_block, r),
                                     h_sem(own_block, r))

    def local_weights(part):
        return pltpu.make_async_copy(
            weights.at[:, pl.ds(pl.multiple_of(part * D + my_group * WIDTH, WIDTH), WIDTH)],
            wbuf.at[part, rows_of(own_piece, core), :], misc.at[2 + part])

    for part in range(3):
        local_weights(part).start()

    @pl.when(across == 0)
    def _():
        for r in range(len(ROUNDS)):
            local_hidden(r).start()

    prod[0:8, :] = jnp.zeros((8, WIDTH), jnp.float32)

    barrier = pltpu.get_barrier_semaphore()
    greeted = [device(mx, my, z, core) for mx, my in mates_to[1:]]
    greeted += [z_to[1], z_to[-1], sibling, partner,
                device(x, y, above, 1 - core), device(x, y, below, 1 - core)]
    for to in greeted:
        pl.semaphore_signal(barrier, inc=1, device_id=to, device_id_type=MESH)
    pl.semaphore_wait(barrier, len(greeted))

    def all_to_all(i):
        mx, my = mates_to[i]
        for part in range(3):
            columns = pl.ds(pl.multiple_of(part * D + (mx * 4 + my) * WIDTH, WIDTH), WIDTH)
            copy(weights.at[:, columns], wbuf.at[part, rows_of(own_piece, core), :],
                 send.at[0], wsem.at[own_piece], device(mx, my, z, core)).start()

    @pl.when(across == 1)
    def _():
        for r in range(len(ROUNDS)):
            rows = pl.ds(*ROUNDS[r])
            copy(hidden.at[rows, :], h_ref(own_block, r), send.at[5],
                 h_sem(own_block, r), sibling).start()

    def own_weights(i):
        mx, my = mates[i]
        piece = piece_of(mx, my, z)
        if i == 0:
            for part in range(3):
                local_weights(part).wait()
        else:
            w_wait(piece)
        w_send(piece, z_to[1], 1)
        w_send(piece, z_to[-1], 1)
        w_sib(piece, ORDER[i][1] % 2)

    def near_weights(i):
        mx, my = mates[i]
        piece = piece_of(mx, my, below)
        w_wait(piece)
        if i % 2 == 0:
            w_send(piece, z_to[1], 1)
        w_sib(piece, 6 + ORDER[i][1] % 2)
        piece = piece_of(mx, my, above)
        w_wait(piece)
        if i % 2 == 1:
            w_send(piece, z_to[-1], 1)
        w_sib(piece, 2 + ORDER[i][1] % 2)

    def far_weights(i):
        mx, my = mates[i]
        piece = piece_of(mx, my, (z + 2) % 4)
        w_wait(piece)
        w_sib(piece, 4 + ORDER[i][1] % 2)

    yh_down, yh_up = down // 2, up // 2

    def hidden0(r):
        @pl.when(across == 0)
        def _():
            a, b = block(x, y_hi, 0), block(x, y_hi, 1)
            h_wait(a, r)
            h_x(a, r)
            h_wait(b, r)
            h_y(b, r)

    def hidden0b(r):
        @pl.when(across == 0)
        def _():
            h_y(block(x, y_hi, 0), r)
            h_x(block(x, y_hi, 1), r)

    def hidden1(r):
        @pl.when(across == 0)
        def _():
            a = block(left, y_hi, 0)
            h_wait(a, r)
            if r % 2 == 0:
                pass_on(x_to, 3, 1, a, r)
            h_y(a, r)
            a = block(right, y_hi, 0)
            h_wait(a, r)
            if r % 2 == 1:
                pass_on(x_to, 3, -1, a, r)
            h_y(a, r)

        @pl.when(across == 1)
        def _():
            b = block(x, yh_down, 1)
            h_wait(b, r)
            if r % 2 == 0:
                pass_on(y_to, 4, 1, b, r)
            h_x(b, r)
            b = block(x, yh_up, 1)
            h_wait(b, r)
            if r % 2 == 1:
                pass_on(y_to, 4, -1, b, r)
            h_x(b, r)

    def hidden2(r):
        @pl.when(across == 0)
        def _():
            a = block((x + 2) % 4, y_hi, 0)
            h_wait(a, r)
            h_y(a, r)
            b = block(x, 1 - y_hi, 1)
            h_wait(b, r)
            h_x(b, r)

    xs_steps = (x, left, right, (x + 2) % 4)

    def hidden3a(m, r):
        @pl.when(across == 1)
        def _():
            a = block(xs_steps[m], yh_down, 0)
            h_wait(a, r)
            if (m + r) % 2 == 0:
                pass_on(y_to, 4, 1, a, r)
            a = block(xs_steps[m], yh_up, 0)
            h_wait(a, r)
            if (m + r) % 2 == 1:
                pass_on(y_to, 4, -1, a, r)

    def hidden3b(r):
        for yh in range(2):
            b = block(left, yh, 1)
            h_wait(b, r)
            if (yh + r) % 2 == 0:
                pass_on(x_to, 3, 1, b, r)
            b = block(right, yh, 1)
            h_wait(b, r)
            if (yh + r) % 2 == 1:
                pass_on(x_to, 3, -1, b, r)

    def hidden4a(m, r):
        @pl.when(across == 0)
        def _():
            h_wait(block(xs_steps[m], 1 - y_hi, 0), r)

    def hidden4b(r):
        for yh in range(2):
            h_wait(block((x + 2) % 4, yh, 1), r)

    def make_taps():
        bank8[0:TAPS, :] = bank[...]
        bank8[TAPS:, :] = jnp.zeros((8 - TAPS, FILTERS), jnp.float32)

        @pl.when(across == 0)
        def _():
            groups = WIDTH // GROUP
            filters = lax.broadcasted_iota(jnp.int32, (FILTERS, groups), 0)
            selector = (filters == assigned[...]).astype(jnp.float32)
            picked = jnp.dot(bank8[...], selector, precision=lax.Precision.HIGHEST,
                             preferred_element_type=jnp.float32)
            owner = lax.broadcasted_iota(jnp.int32, (groups, WIDTH), 1) // GROUP
            member = lax.broadcasted_iota(jnp.int32, (groups, WIDTH), 0)
            taps[...] = jnp.dot(picked, (owner == member).astype(jnp.float32),
                                precision=lax.Precision.HIGHEST,
                                preferred_element_type=jnp.float32)
            copy(taps, taps, send.at[6], misc.at[0], sibling).start()

        @pl.when(across == 1)
        def _():
            copy(taps, taps, send.at[6], misc.at[0], sibling).wait_recv()

    codes = [(kind == "x") * 32 + r * 8 + step * 2 + half for kind, r, step, half in DOTS]
    words = [sum(code << 6 * i for i, code in enumerate(codes[first:first + 5]))
             for first in range(0, len(codes), 5)]

    def dot(s):
        word = jnp.int32(words[0])
        for i in range(1, len(words)):
            word = jnp.where(s >= 5 * i, jnp.int32(words[i]), word)
        code = lax.shift_right_logical(word, 6 * (s % 5)) % 64
        by_x, r, step, half = code // 32, code // 8 % 4, code // 2 % 4, code % 2
        z_block = ((y_lo + half) % 2) * 4 + (z + step) % 4
        shift = jnp.where(step == 0, 0, jnp.where(step == 1, 3, step - 1))
        x_block = ((x + shift) % 4) * 2 + half
        b = jnp.where(by_x == 1, x_block, z_block)
        rows = pl.ds(pl.multiple_of((r + 3) % 4 * CHUNK, CHUNK), CHUNK)
        depth = pl.ds(pl.multiple_of(b * 1024, 1024), 1024)
        left_side = jnp.concatenate([hbuf[2 * b, rows, :], hbuf[2 * b + 1, rows, :]], axis=1)
        for part in range(3):
            acc[rows, part * WIDTH:(part + 1) * WIDTH] += jnp.dot(
                left_side, wbuf[part, depth, :], preferred_element_type=jnp.float32)

    SUB = 32

    def products(base):
        def step(i, _):
            rows = pl.ds(pl.multiple_of(base + i * SUB, SUB), SUB)
            prod[pl.ds(pl.multiple_of(base + i * SUB + 8, 8), SUB), :] = (
                acc[rows, WIDTH:2 * WIDTH] * acc[rows, 2 * WIDTH:])
            return 0
        lax.fori_loop(0, CHUNK // SUB, step, 0)

    def filtered(base, count, size):
        def step(i, _):
            first = pl.multiple_of(base + i * size, size)
            near = prod[pl.ds(first, size + 8), :]
            total = jnp.zeros((size, WIDTH), jnp.float32)
            for j in range(TAPS):
                total = total + taps[j:j + 1, :] * near[8 - j:8 - j + size, :]
            rows = pl.ds(first, size)
            stage[rows, :] = (acc[rows, 0:WIDTH] * total).astype(jnp.bfloat16)
            return 0
        lax.fori_loop(0, count, step, 0)

    def out_send(first, count, sem):
        src, dst = stage.at[pl.ds(first, count), :], out.at[pl.ds(first, count), :]

        @pl.when(across == 0)
        def _():
            pltpu.make_async_copy(src, dst, misc.at[sem]).start()

        @pl.when(across == 1)
        def _():
            copy(src, dst, send.at[8], misc.at[sem], partner).start()

    def out_wait(first, count, sem):
        src, dst = stage.at[pl.ds(first, count), :], out.at[pl.ds(first, count), :]

        @pl.when(across == 0)
        def _():
            pltpu.make_async_copy(src, dst, misc.at[sem]).wait()

        @pl.when(across == 1)
        def _():
            copy(src, dst, send.at[8], misc.at[sem], partner).wait_recv()

    halo_from, halo_to = prod.at[pl.ds(TOKENS, 8), :], prod.at[pl.ds(0, 8), :]
    last_window = (z == 3) & (core == 1)
    first_window = (z == 0) & (core == 0)
    next_core = jnp.where(z == 3, 1 - core, core)

    def halo():
        return copy(halo_from, halo_to, send.at[7], misc.at[1], device(x, y, above, next_core))

    def epilogue0():
        products(3 * CHUNK)

        @pl.when(jnp.logical_not(last_window))
        def _():
            halo().start()

        filtered(3 * CHUNK + 32, 7, 32)
        out_send(3 * CHUNK + 32, CHUNK - 32, 5)

    def epilogue1():
        products(0)

        @pl.when(jnp.logical_not(first_window))
        def _():
            halo().wait_recv()

        filtered(0, 8, 32)
        out_send(0, CHUNK, 6)

    def epilogue2():
        products(CHUNK)
        filtered(CHUNK, 8, 32)
        out_send(CHUNK, CHUNK, 7)

    def epilogue3():
        products(2 * CHUNK)
        filtered(2 * CHUNK, 4, 32)
        out_send(2 * CHUNK, 128, 8)
        filtered(2 * CHUNK + 128, 5, 32)
        out_send(2 * CHUNK + 128, 160, 9)

    def zero_acc():
        def step(i, _):
            rows = pl.ds(pl.multiple_of(i * 32, 32), 32)
            acc[rows, :] = jnp.zeros((32, 3 * WIDTH), jnp.float32)
            return 0
        lax.fori_loop(0, TOKENS // 32, step, 0)

    run = {"taps": make_taps, "zero": zero_acc, "all": all_to_all, "own": own_weights, "near": near_weights, "far": far_weights, "sib": sib_wait,
           "h0": hidden0, "h0b": hidden0b, "h1": hidden1, "h2": hidden2, "h3a": hidden3a, "h3b": hidden3b,
           "h4a": hidden4a, "h4b": hidden4b}
    before = timeline()
    last_dot = {r: max(s for s in range(len(DOTS)) if DOTS[s][1] == r) for r in range(CHUNKS)}

    def slot_step(s, _):
        for k in range(len(DOTS)):
            @pl.when(s == k)
            def _(k=k):
                for name, *args in before[k]:
                    run[name](*args)
                for r, epilogue in enumerate((epilogue0, epilogue1, epilogue2)):
                    if k == max(last_dot[i] for i in range(r + 1)) + 1:
                        epilogue()
        dot(s)
        return 0
    lax.fori_loop(0, len(DOTS), slot_step, 0)
    epilogue3()

    out_wait(3 * CHUNK + 32, CHUNK - 32, 5)
    out_wait(0, CHUNK, 6)
    out_wait(CHUNK, CHUNK, 7)
    out_wait(2 * CHUNK, 128, 8)
    out_wait(2 * CHUNK + 128, 160, 9)

    def sent(ref, sem):
        copy(ref, ref, send.at[sem], misc.at[0], sibling).wait_send()

    sent(wbuf.at[:, pl.ds(0, 15 * ROWS), :], 0)
    sent(wbuf.at[:, pl.ds(0, 48 * ROWS), :], 1)
    sent(wbuf.at[:, pl.ds(0, 64 * ROWS), :], 2)

    @pl.when(across == 0)
    def _():
        sent(hbuf.at[pl.ds(0, 9)], 3)
        sent(hbuf.at[pl.ds(0, 10)], 4)
        sent(taps, 6)

    @pl.when(across == 1)
    def _():
        sent(hbuf.at[pl.ds(0, 6)], 3)
        sent(hbuf.at[pl.ds(0, 5)], 4)
        sent(hidden, 5)
        sent(stage, 8)

    @pl.when(jnp.logical_not(last_window))
    def _():
        halo().wait_send()


def on_device(hidden, in_weights, filter_bank, assignment):
    any_space = pl.BlockSpec(memory_space=pl.ANY)
    vmem = pl.BlockSpec(memory_space=pltpu.VMEM)
    return pl.pallas_call(
        kernel,
        name="hyena",
        out_shape=jax.ShapeDtypeStruct((TOKENS, WIDTH), jnp.bfloat16),
        in_specs=[any_space, any_space, vmem, vmem],
        out_specs=any_space,
        scratch_shapes=[
            pltpu.VMEM((16, TOKENS, WIDTH), jnp.bfloat16),
            pltpu.VMEM((3, D, WIDTH), jnp.bfloat16),
            pltpu.VMEM((TOKENS, 3 * WIDTH), jnp.float32),
            pltpu.VMEM((TOKENS + 8, WIDTH), jnp.float32),
            pltpu.VMEM((TOKENS, WIDTH), jnp.bfloat16),
            pltpu.VMEM((8, WIDTH), jnp.float32),
            pltpu.VMEM((8, FILTERS), jnp.float32),
            pltpu.SemaphoreType.DMA((16 * len(ROUNDS),)),
            pltpu.SemaphoreType.DMA((64,)),
            pltpu.SemaphoreType.DMA((8,)),
            pltpu.SemaphoreType.DMA((10,)),
            pltpu.SemaphoreType.DMA((10,)),
        ],
        compiler_params=pltpu.CompilerParams(
            collective_id=0, has_side_effects=True, vmem_limit_bytes=60 * 2**20),
        cost_estimate=pl.CostEstimate(
            flops=2 * TOKENS * D * 3 * WIDTH, bytes_accessed=44 * 2**20, transcendentals=0),
    )(hidden, in_weights, filter_bank, assignment[None, :])


def solution(mesh):
    in_specs = (P("seq", "chan"), P(("seq", "chan"), None), P(), P("chan"))
    return jax.shard_map(
        on_device, mesh=mesh, in_specs=in_specs, out_specs=P("seq", "chan"), check_vma=False)
```

```python
import jax
import jax.numpy as jnp
from jax import lax
from jax.experimental import pallas as pl
from jax.experimental.pallas import tpu as pltpu
from jax.sharding import PartitionSpec as P

D = 8192
GROUP = 16
TAPS = 7
FILTERS = 512
TOKENS = 1024
WIDTH = 512
ROWS = 64
CHUNK = 256
CHUNKS = TOKENS // CHUNK
MESH = pl.DeviceIdType.MESH

ROUNDS = ((768, 256), (0, 256), (256, 256), (512, 256))
ORDER = ((0, 0), (1, 2), (3, 2), (2, 0), (1, 0), (3, 0), (0, 2), (2, 2),
         (1, 1), (3, 3), (1, 3), (3, 1), (0, 1), (0, 3), (2, 1), (2, 3))
STARTS = (15.0, 37.0, 60.0, 81.0)
STAGES = (0.0, 6.54, 23.09, 34.44, 49.63)
LAST = (12.84, 25.44, 35.22, 44.3, 71.25)
SPREAD = (2.51, 2.56)
SPLIT = 21.05
ALL = (0, 0.5)
OWN = (3.64, 1.48)
NEAR = (19.06, 1.08, 5.8)
FAR = (73.66, 4.68)
DOT = 1.7

HOPS = (0, 1, 3, 2)
DOTS = (
    ("z", 0, 0, 0), ("z", 0, 1, 0), ("z", 0, 3, 0), ("z", 1, 0, 0),
    ("z", 1, 1, 0), ("z", 1, 3, 0), ("z", 0, 0, 1), ("z", 0, 1, 1),
    ("z", 0, 3, 1), ("z", 1, 0, 1), ("z", 1, 1, 1), ("z", 1, 3, 1),
    ("z", 0, 2, 0), ("z", 1, 2, 0), ("z", 2, 0, 0), ("z", 2, 0, 1),
    ("z", 2, 1, 0), ("z", 2, 1, 1), ("z", 2, 3, 0), ("z", 2, 3, 1),
    ("z", 2, 2, 0), ("z", 0, 2, 1), ("z", 1, 2, 1), ("z", 2, 2, 1),
    ("x", 3, 0, 1), ("x", 3, 0, 0), ("x", 3, 1, 0), ("x", 3, 1, 1),
    ("x", 3, 2, 0), ("x", 3, 2, 1), ("x", 3, 3, 0), ("x", 3, 3, 1),
)


def hidden_needs(m, r):
    return [("h3a", m, r), ("h4a", m, r)] + [
        [("h1", r), ("h2", r)], [("h1", r), ("h3b", r)], [("h1", r), ("h3b", r)],
        [("h2", r), ("h4b", r)]][m]


def timeline():
    when = {("taps",): 30.0, ("zero",): 33.0}
    for i in range(16):
        if i:
            when["all", i] = ALL[0] + ALL[1] * i
        when["own", i] = OWN[0] + OWN[1] * i
        when["near", i] = max(NEAR[0], NEAR[1] + NEAR[2] * i)
        when["far", i] = FAR[0] + FAR[1] * (i // 2 + 1)
    for r, start in enumerate(STARTS):
        stages = LAST if r == CHUNKS - 1 else STAGES
        when["h0b", r] = start + stages[0] + SPLIT
        for index in range(3):
            when["h%d" % index, r] = start + stages[index]
        for m in range(4):
            when["h3a", m, r] = start + stages[3] + SPREAD[0] * m
            when["h4a", m, r] = start + stages[4] + SPREAD[1] * m
        when["h3b", r] = start + stages[3] + SPREAD[0] * 1.5
        when["h4b", r] = start + stages[4] + SPREAD[1] * 2.5
    kinds = {0: "own", 1: "near", 3: "near", 2: "far"}
    for hop in HOPS:
        for half in range(2):
            last = max(when[kinds[hop], i] for i in range(16) if ORDER[i][1] % 2 == half)
            when["sib", hop, half] = last + 3.0

    slots, placed, clock = [], set(), 0.0
    names = list(when)
    for kind, r, step, half in DOTS:
        if kind == "z":
            needs = [key for m in range(4) for key in hidden_needs(m, r)]
            needs += [("sib", step, half)]
        else:
            needs = hidden_needs(step, r) + [
                ("sib", hop, h) for hop in HOPS for h in range(2)]
        clock = max([clock + DOT] + [when[key] for key in needs])
        ready = [key for key in names if when[key] <= clock and key not in placed]
        ready = sorted(ready, key=when.get)
        placed.update(ready)
        slots.append(ready)
    rest = [key for key in names if key not in placed]
    assert not rest
    return slots


def device(x, y, z, core):
    return ((y % 2) * 4 + z, x * 4 + (y // 2) * 2 + core)


def kernel(hidden, weights, bank, assigned, out, hbuf, wbuf, acc, prod, stage, taps, bank8,
           hsem, wsem, sibsem, misc, send):
    seq, chan = lax.axis_index("seq"), lax.axis_index("chan")
    x, y, z, core = chan // 4, (chan // 2 % 2) * 2 + seq // 4, seq % 4, chan % 2
    y_hi, y_lo = y // 2, y % 2
    across = (y_lo + core) % 2
    left, right = (x + 3) % 4, (x + 1) % 4
    down, up = (y + 3) % 4, (y + 1) % 4
    below, above = (z + 3) % 4, (z + 1) % 4
    sibling = device(x, y, z, 1 - core)
    partner = device(x, y + 1 - 2 * y_lo, z, 1 - core)
    x_to = {1: device(right, y, z, core), -1: device(left, y, z, core)}
    y_to = {1: device(x, up, z, core), -1: device(x, down, z, core)}
    z_to = {1: device(x, y, above, core), -1: device(x, y, below, core)}

    sign = 1 - 2 * core
    mates_to = [((x + sign * dx + 4) % 4, (y + sign * dy + 4) % 4) for dx, dy in ORDER]
    mates = [((x - sign * dx + 4) % 4, (y - sign * dy + 4) % 4) for dx, dy in ORDER]

    def copy(src, dst, send_sem, recv_sem, to):
        return pltpu.make_async_remote_copy(
            src_ref=src, dst_ref=dst, send_sem=send_sem, recv_sem=recv_sem,
            device_id=to, device_id_type=MESH)

    def rows_of(piece, owner):
        return pl.ds(pl.multiple_of((piece * 2 + owner) * ROWS, ROWS), ROWS)

    def piece_of(xs, ys, zs):
        return ((ys % 2) * 4 + zs) * 8 + xs * 2 + ys // 2

    def w_send(piece, to, sem):
        ref = wbuf.at[:, rows_of(piece, core), :]
        copy(ref, ref, send.at[sem], wsem.at[piece], to).start()

    def w_sib(piece, group):
        ref = wbuf.at[:, rows_of(piece, core), :]
        copy(ref, ref, send.at[2], sibsem.at[group], sibling).start()

    def w_wait(piece):
        ref = wbuf.at[:, rows_of(piece, core), :]
        copy(ref, ref, send.at[0], wsem.at[piece], sibling).wait_recv()

    def sib_wait(hop, half):
        ref = wbuf.at[:, pl.ds(0, 8 * ROWS), :]
        copy(ref, ref, send.at[2], sibsem.at[2 * hop + half], sibling).wait_recv()

    def block(xs, yh, ks):
        return xs * 4 + yh * 2 + ks

    def h_ref(b, r):
        return hbuf.at[b, pl.ds(*ROUNDS[r]), :]

    def h_sem(b, r):
        return hsem.at[b * len(ROUNDS) + r]

    def h_send(b, r, to, sem):
        copy(h_ref(b, r), h_ref(b, r), send.at[sem], h_sem(b, r), to).start()

    def h_x(b, r):
        for side in (1, -1):
            h_send(b, r, x_to[side], 3)

    def h_y(b, r):
        for side in (1, -1):
            h_send(b, r, y_to[side], 4)

    def pass_on(to, sem, side, b, r):
        h_send(b, r, to[side], sem)

    def h_wait(b, r):
        copy(h_ref(b, r), h_ref(b, r), send.at[3], h_sem(b, r), sibling).wait_recv()

    own_block = block(x, y_hi, core)
    own_piece = piece_of(x, y, z)
    my_group = x * 4 + y

    def local_hidden(r):
        rows = pl.ds(*ROUNDS[r])
        return pltpu.make_async_copy(hidden.at[rows, :], h_ref(own_block, r),
                                     h_sem(own_block, r))

    def local_weights(part):
        return pltpu.make_async_copy(
            weights.at[:, pl.ds(pl.multiple_of(part * D + my_group * WIDTH, WIDTH), WIDTH)],
            wbuf.at[part, rows_of(own_piece, core), :], misc.at[2 + part])

    for part in range(3):
        local_weights(part).start()

    @pl.when(across == 0)
    def _():
        for r in range(len(ROUNDS)):
            local_hidden(r).start()

    prod[0:8, :] = jnp.zeros((8, WIDTH), jnp.float32)

    barrier = pltpu.get_barrier_semaphore()
    greeted = [device(mx, my, z, core) for mx, my in mates_to[1:]]
    greeted += [z_to[1], z_to[-1], sibling, partner,
                device(x, y, above, 1 - core), device(x, y, below, 1 - core)]
    for to in greeted:
        pl.semaphore_signal(barrier, inc=1, device_id=to, device_id_type=MESH)
    pl.semaphore_wait(barrier, len(greeted))

    def all_to_all(i):
        mx, my = mates_to[i]
        for part in range(3):
            columns = pl.ds(pl.multiple_of(part * D + (mx * 4 + my) * WIDTH, WIDTH), WIDTH)
            copy(weights.at[:, columns], wbuf.at[part, rows_of(own_piece, core), :],
                 send.at[0], wsem.at[own_piece], device(mx, my, z, core)).start()

    @pl.when(across == 1)
    def _():
        for r in range(len(ROUNDS)):
            rows = pl.ds(*ROUNDS[r])
            copy(hidden.at[rows, :], h_ref(own_block, r), send.at[5],
                 h_sem(own_block, r), sibling).start()

    def own_weights(i):
        mx, my = mates[i]
        piece = piece_of(mx, my, z)
        if i == 0:
            for part in range(3):
                local_weights(part).wait()
        else:
            w_wait(piece)
        w_send(piece, z_to[1], 1)
        w_send(piece, z_to[-1], 1)
        w_sib(piece, ORDER[i][1] % 2)

    def near_weights(i):
        mx, my = mates[i]
        piece = piece_of(mx, my, below)
        w_wait(piece)
        if i % 2 == 0:
            w_send(piece, z_to[1], 1)
        w_sib(piece, 6 + ORDER[i][1] % 2)
        piece = piece_of(mx, my, above)
        w_wait(piece)
        if i % 2 == 1:
            w_send(piece, z_to[-1], 1)
        w_sib(piece, 2 + ORDER[i][1] % 2)

    def far_weights(i):
        mx, my = mates[i]
        piece = piece_of(mx, my, (z + 2) % 4)
        w_wait(piece)
        w_sib(piece, 4 + ORDER[i][1] % 2)

    yh_down, yh_up = down // 2, up // 2

    def hidden0(r):
        @pl.when(across == 0)
        def _():
            a, b = block(x, y_hi, 0), block(x, y_hi, 1)
            h_wait(a, r)
            h_x(a, r)
            h_wait(b, r)
            h_y(b, r)

    def hidden0b(r):
        @pl.when(across == 0)
        def _():
            h_y(block(x, y_hi, 0), r)
            h_x(block(x, y_hi, 1), r)

    def hidden1(r):
        @pl.when(across == 0)
        def _():
            a = block(left, y_hi, 0)
            h_wait(a, r)
            if r % 2 == 0:
                pass_on(x_to, 3, 1, a, r)
            h_y(a, r)
            a = block(right, y_hi, 0)
            h_wait(a, r)
            if r % 2 == 1:
                pass_on(x_to, 3, -1, a, r)
            h_y(a, r)

        @pl.when(across == 1)
        def _():
            b = block(x, yh_down, 1)
            h_wait(b, r)
            if r % 2 == 0:
                pass_on(y_to, 4, 1, b, r)
            h_x(b, r)
            b = block(x, yh_up, 1)
            h_wait(b, r)
            if r % 2 == 1:
                pass_on(y_to, 4, -1, b, r)
            h_x(b, r)

    def hidden2(r):
        @pl.when(across == 0)
        def _():
            a = block((x + 2) % 4, y_hi, 0)
            h_wait(a, r)
            h_y(a, r)
            b = block(x, 1 - y_hi, 1)
            h_wait(b, r)
            h_x(b, r)

    xs_steps = (x, left, right, (x + 2) % 4)

    def hidden3a(m, r):
        @pl.when(across == 1)
        def _():
            a = block(xs_steps[m], yh_down, 0)
            h_wait(a, r)
            if (m + r) % 2 == 0:
                pass_on(y_to, 4, 1, a, r)
            a = block(xs_steps[m], yh_up, 0)
            h_wait(a, r)
            if (m + r) % 2 == 1:
                pass_on(y_to, 4, -1, a, r)

    def hidden3b(r):
        for yh in range(2):
            b = block(left, yh, 1)
            h_wait(b, r)
            if (yh + r) % 2 == 0:
                pass_on(x_to, 3, 1, b, r)
            b = block(right, yh, 1)
            h_wait(b, r)
            if (yh + r) % 2 == 1:
                pass_on(x_to, 3, -1, b, r)

    def hidden4a(m, r):
        @pl.when(across == 0)
        def _():
            h_wait(block(xs_steps[m], 1 - y_hi, 0), r)

    def hidden4b(r):
        for yh in range(2):
            h_wait(block((x + 2) % 4, yh, 1), r)

    def make_taps():
        bank8[0:TAPS, :] = bank[...]
        bank8[TAPS:, :] = jnp.zeros((8 - TAPS, FILTERS), jnp.float32)

        @pl.when(across == 0)
        def _():
            groups = WIDTH // GROUP
            filters = lax.broadcasted_iota(jnp.int32, (FILTERS, groups), 0)
            selector = (filters == assigned[...]).astype(jnp.float32)
            picked = jnp.dot(bank8[...], selector, precision=lax.Precision.HIGHEST,
                             preferred_element_type=jnp.float32)
            owner = lax.broadcasted_iota(jnp.int32, (groups, WIDTH), 1) // GROUP
            member = lax.broadcasted_iota(jnp.int32, (groups, WIDTH), 0)
            taps[...] = jnp.dot(picked, (owner == member).astype(jnp.float32),
                                precision=lax.Precision.HIGHEST,
                                preferred_element_type=jnp.float32)
            copy(taps, taps, send.at[6], misc.at[0], sibling).start()

        @pl.when(across == 1)
        def _():
            copy(taps, taps, send.at[6], misc.at[0], sibling).wait_recv()

    codes = [(kind == "x") * 32 + r * 8 + step * 2 + half for kind, r, step, half in DOTS]
    words = [sum(code << 6 * i for i, code in enumerate(codes[first:first + 5]))
             for first in range(0, len(codes), 5)]

    def dot(s):
        word = jnp.int32(words[0])
        for i in range(1, len(words)):
            word = jnp.where(s >= 5 * i, jnp.int32(words[i]), word)
        code = lax.shift_right_logical(word, 6 * (s % 5)) % 64
        by_x, r, step, half = code // 32, code // 8 % 4, code // 2 % 4, code % 2
        z_block = ((y_lo + half) % 2) * 4 + (z + step) % 4
        shift = jnp.where(step == 0, 0, jnp.where(step == 1, 3, step - 1))
        x_block = ((x + shift) % 4) * 2 + half
        b = jnp.where(by_x == 1, x_block, z_block)
        rows = pl.ds(pl.multiple_of((r + 3) % 4 * CHUNK, CHUNK), CHUNK)
        depth = pl.ds(pl.multiple_of(b * 1024, 1024), 1024)
        left_side = jnp.concatenate([hbuf[2 * b, rows, :], hbuf[2 * b + 1, rows, :]], axis=1)
        for part in range(3):
            acc[rows, part * WIDTH:(part + 1) * WIDTH] += jnp.dot(
                left_side, wbuf[part, depth, :], preferred_element_type=jnp.float32)

    SUB = 32

    def products(base):
        def step(i, _):
            rows = pl.ds(pl.multiple_of(base + i * SUB, SUB), SUB)
            prod[pl.ds(pl.multiple_of(base + i * SUB + 8, 8), SUB), :] = (
                acc[rows, WIDTH:2 * WIDTH] * acc[rows, 2 * WIDTH:])
            return 0
        lax.fori_loop(0, CHUNK // SUB, step, 0)

    def filtered(base, count, size):
        def step(i, _):
            first = pl.multiple_of(base + i * size, size)
            near = prod[pl.ds(first, size + 8), :]
            total = jnp.zeros((size, WIDTH), jnp.float32)
            for j in range(TAPS):
                total = total + taps[j:j + 1, :] * near[8 - j:8 - j + size, :]
            rows = pl.ds(first, size)
            stage[rows, :] = (acc[rows, 0:WIDTH] * total).astype(jnp.bfloat16)
            return 0
        lax.fori_loop(0, count, step, 0)

    def out_send(first, count, sem):
        src, dst = stage.at[pl.ds(first, count), :], out.at[pl.ds(first, count), :]

        @pl.when(across == 0)
        def _():
            pltpu.make_async_copy(src, dst, misc.at[sem]).start()

        @pl.when(across == 1)
        def _():
            copy(src, dst, send.at[8], misc.at[sem], partner).start()

    def out_wait(first, count, sem):
        src, dst = stage.at[pl.ds(first, count), :], out.at[pl.ds(first, count), :]

        @pl.when(across == 0)
        def _():
            pltpu.make_async_copy(src, dst, misc.at[sem]).wait()

        @pl.when(across == 1)
        def _():
            copy(src, dst, send.at[8], misc.at[sem], partner).wait_recv()

    halo_from, halo_to = prod.at[pl.ds(TOKENS, 8), :], prod.at[pl.ds(0, 8), :]
    last_window = (z == 3) & (core == 1)
    first_window = (z == 0) & (core == 0)
    next_core = jnp.where(z == 3, 1 - core, core)

    def halo():
        return copy(halo_from, halo_to, send.at[7], misc.at[1], device(x, y, above, next_core))

    def epilogue0():
        products(3 * CHUNK)

        @pl.when(jnp.logical_not(last_window))
        def _():
            halo().start()

        filtered(3 * CHUNK + 32, 7, 32)
        out_send(3 * CHUNK + 32, CHUNK - 32, 5)

    def epilogue1():
        products(0)

        @pl.when(jnp.logical_not(first_window))
        def _():
            halo().wait_recv()

        filtered(0, 8, 32)
        out_send(0, CHUNK, 6)

    def epilogue2():
        products(CHUNK)
        filtered(CHUNK, 8, 32)
        out_send(CHUNK, CHUNK, 7)

    def epilogue3():
        products(2 * CHUNK)
        filtered(2 * CHUNK, 4, 32)
        out_send(2 * CHUNK, 128, 8)
        filtered(2 * CHUNK + 128, 5, 32)
        out_send(2 * CHUNK + 128, 160, 9)

    def zero_acc():
        def step(i, _):
            rows = pl.ds(pl.multiple_of(i * 32, 32), 32)
            acc[rows, :] = jnp.zeros((32, 3 * WIDTH), jnp.float32)
            return 0
        lax.fori_loop(0, TOKENS // 32, step, 0)

    run = {"taps": make_taps, "zero": zero_acc, "all": all_to_all, "own": own_weights, "near": near_weights, "far": far_weights, "sib": sib_wait,
           "h0": hidden0, "h0b": hidden0b, "h1": hidden1, "h2": hidden2, "h3a": hidden3a, "h3b": hidden3b,
           "h4a": hidden4a, "h4b": hidden4b}
    before = timeline()
    last_dot = {r: max(s for s in range(len(DOTS)) if DOTS[s][1] == r) for r in range(CHUNKS)}

    def slot_step(s, _):
        for k in range(len(DOTS)):
            @pl.when(s == k)
            def _(k=k):
                for name, *args in before[k]:
                    run[name](*args)
                for r, epilogue in enumerate((epilogue0, epilogue1, epilogue2)):
                    if k == max(last_dot[i] for i in range(r + 1)) + 1:
                        epilogue()
        dot(s)
        return 0
    lax.fori_loop(0, len(DOTS), slot_step, 0)
    epilogue3()

    out_wait(3 * CHUNK + 32, CHUNK - 32, 5)
    out_wait(0, CHUNK, 6)
    out_wait(CHUNK, CHUNK, 7)
    out_wait(2 * CHUNK, 128, 8)
    out_wait(2 * CHUNK + 128, 160, 9)

    def sent(ref, sem):
        copy(ref, ref, send.at[sem], misc.at[0], sibling).wait_send()

    sent(wbuf.at[:, pl.ds(0, 15 * ROWS), :], 0)
    sent(wbuf.at[:, pl.ds(0, 48 * ROWS), :], 1)
    sent(wbuf.at[:, pl.ds(0, 64 * ROWS), :], 2)

    @pl.when(across == 0)
    def _():
        sent(hbuf.at[pl.ds(0, 9)], 3)
        sent(hbuf.at[pl.ds(0, 10)], 4)
        sent(taps, 6)

    @pl.when(across == 1)
    def _():
        sent(hbuf.at[pl.ds(0, 6)], 3)
        sent(hbuf.at[pl.ds(0, 5)], 4)
        sent(hidden, 5)
        sent(stage, 8)

    @pl.when(jnp.logical_not(last_window))
    def _():
        halo().wait_send()


def on_device(hidden, in_weights, filter_bank, assignment):
    any_space = pl.BlockSpec(memory_space=pl.ANY)
    vmem = pl.BlockSpec(memory_space=pltpu.VMEM)
    return pl.pallas_call(
        kernel,
        name="hyena",
        out_shape=jax.ShapeDtypeStruct((TOKENS, WIDTH), jnp.bfloat16),
        in_specs=[any_space, any_space, vmem, vmem],
        out_specs=any_space,
        scratch_shapes=[
            pltpu.VMEM((16, TOKENS, WIDTH), jnp.bfloat16),
            pltpu.VMEM((3, D, WIDTH), jnp.bfloat16),
            pltpu.VMEM((TOKENS, 3 * WIDTH), jnp.float32),
            pltpu.VMEM((TOKENS + 8, WIDTH), jnp.float32),
            pltpu.VMEM((TOKENS, WIDTH), jnp.bfloat16),
            pltpu.VMEM((8, WIDTH), jnp.float32),
            pltpu.VMEM((8, FILTERS), jnp.float32),
            pltpu.SemaphoreType.DMA((16 * len(ROUNDS),)),
            pltpu.SemaphoreType.DMA((64,)),
            pltpu.SemaphoreType.DMA((8,)),
            pltpu.SemaphoreType.DMA((10,)),
            pltpu.SemaphoreType.DMA((10,)),
        ],
        compiler_params=pltpu.CompilerParams(
            collective_id=0, has_side_effects=True, vmem_limit_bytes=60 * 2**20),
        cost_estimate=pl.CostEstimate(
            flops=2 * TOKENS * D * 3 * WIDTH, bytes_accessed=44 * 2**20, transcendentals=0),
    )(hidden, in_weights, filter_bank, assignment[None, :])


def solution(mesh):
    in_specs = (P("seq", "chan"), P(("seq", "chan"), None), P(), P("chan"))
    return jax.shard_map(
        on_device, mesh=mesh, in_specs=in_specs, out_specs=P("seq", "chan"), check_vma=False)
```

```python
import jax
import jax.numpy as jnp
from jax import lax
from jax.experimental import pallas as pl
from jax.experimental.pallas import tpu as pltpu
from jax.sharding import PartitionSpec as P

D = 8192
GROUP = 16
TAPS = 7
FILTERS = 512
TOKENS = 1024
WIDTH = 512
ROWS = 64
CHUNK = 256
CHUNKS = TOKENS // CHUNK
MESH = pl.DeviceIdType.MESH

ROUNDS = ((768, 256), (0, 256), (256, 256), (512, 256))
ORDER = ((0, 0), (1, 0), (3, 0), (0, 2), (2, 0), (1, 2), (3, 2), (2, 2),
         (0, 1), (0, 3), (1, 1), (3, 3), (1, 3), (3, 1), (2, 1), (2, 3))
STARTS = (15.0, 37.0, 60.0, 81.0)
STAGES = (0.0, 6.54, 23.09, 34.44, 49.63)
LAST = (12.84, 25.44, 35.22, 44.3, 71.25)
SPREAD = (2.51, 2.56)
SPLIT = 21.05
ALL = (0, 0.5)
OWN = (3.64, 1.48)
NEAR = (19.06, 1.08, 5.8)
FAR = (73.66, 4.68)
DOT = 1.7

HOPS = (0, 1, 3, 2)
DOTS = (
    ("z", 0, 0, 0), ("z", 0, 1, 0), ("z", 0, 3, 0), ("z", 1, 0, 0),
    ("z", 1, 1, 0), ("z", 1, 3, 0), ("z", 0, 0, 1), ("z", 0, 1, 1),
    ("z", 0, 3, 1), ("z", 1, 0, 1), ("z", 1, 1, 1), ("z", 1, 3, 1),
    ("z", 0, 2, 0), ("z", 1, 2, 0), ("z", 2, 0, 0), ("z", 2, 0, 1),
    ("z", 2, 1, 0), ("z", 2, 1, 1), ("z", 2, 3, 0), ("z", 2, 3, 1),
    ("z", 2, 2, 0), ("z", 0, 2, 1), ("z", 1, 2, 1), ("z", 2, 2, 1),
    ("x", 3, 0, 1), ("x", 3, 0, 0), ("x", 3, 1, 0), ("x", 3, 1, 1),
    ("x", 3, 2, 0), ("x", 3, 2, 1), ("x", 3, 3, 0), ("x", 3, 3, 1),
)


def hidden_needs(m, r):
    return [("h3a", m, r), ("h4a", m, r)] + [
        [("h1", r), ("h2", r)], [("h1", r), ("h3b", r)], [("h1", r), ("h3b", r)],
        [("h2", r), ("h4b", r)]][m]


def timeline():
    when = {("taps",): 30.0, ("zero",): 33.0}
    for i in range(16):
        if i:
            when["all", i] = ALL[0] + ALL[1] * i
        when["own", i] = OWN[0] + OWN[1] * i
        when["near", i] = max(NEAR[0], NEAR[1] + NEAR[2] * i)
        when["far", i] = FAR[0] + FAR[1] * (i // 2 + 1)
    for r, start in enumerate(STARTS):
        stages = LAST if r == CHUNKS - 1 else STAGES
        when["h0b", r] = start + stages[0] + SPLIT
        for index in range(3):
            when["h%d" % index, r] = start + stages[index]
        for m in range(4):
            when["h3a", m, r] = start + stages[3] + SPREAD[0] * m
            when["h4a", m, r] = start + stages[4] + SPREAD[1] * m
        when["h3b", r] = start + stages[3] + SPREAD[0] * 1.5
        when["h4b", r] = start + stages[4] + SPREAD[1] * 2.5
    kinds = {0: "own", 1: "near", 3: "near", 2: "far"}
    for hop in HOPS:
        for half in range(2):
            last = max(when[kinds[hop], i] for i in range(16) if ORDER[i][1] % 2 == half)
            when["sib", hop, half] = last + 3.0

    slots, placed, clock = [], set(), 0.0
    names = list(when)
    for kind, r, step, half in DOTS:
        if kind == "z":
            needs = [key for m in range(4) for key in hidden_needs(m, r)]
            needs += [("sib", step, half)]
        else:
            needs = hidden_needs(step, r) + [
                ("sib", hop, h) for hop in HOPS for h in range(2)]
        clock = max([clock + DOT] + [when[key] for key in needs])
        ready = [key for key in names if when[key] <= clock and key not in placed]
        ready = sorted(ready, key=when.get)
        placed.update(ready)
        slots.append(ready)
    rest = [key for key in names if key not in placed]
    assert not rest
    return slots


def device(x, y, z, core):
    return ((y % 2) * 4 + z, x * 4 + (y // 2) * 2 + core)


def kernel(hidden, weights, bank, assigned, out, hbuf, wbuf, acc, prod, stage, taps, bank8,
           hsem, wsem, sibsem, misc, send):
    seq, chan = lax.axis_index("seq"), lax.axis_index("chan")
    x, y, z, core = chan // 4, (chan // 2 % 2) * 2 + seq // 4, seq % 4, chan % 2
    y_hi, y_lo = y // 2, y % 2
    across = (y_lo + core) % 2
    left, right = (x + 3) % 4, (x + 1) % 4
    down, up = (y + 3) % 4, (y + 1) % 4
    below, above = (z + 3) % 4, (z + 1) % 4
    sibling = device(x, y, z, 1 - core)
    partner = device(x, y + 1 - 2 * y_lo, z, 1 - core)
    x_to = {1: device(right, y, z, core), -1: device(left, y, z, core)}
    y_to = {1: device(x, up, z, core), -1: device(x, down, z, core)}
    z_to = {1: device(x, y, above, core), -1: device(x, y, below, core)}

    sign = 1 - 2 * core
    mates_to = [((x + sign * dx + 4) % 4, (y + sign * dy + 4) % 4) for dx, dy in ORDER]
    mates = [((x - sign * dx + 4) % 4, (y - sign * dy + 4) % 4) for dx, dy in ORDER]

    def copy(src, dst, send_sem, recv_sem, to):
        return pltpu.make_async_remote_copy(
            src_ref=src, dst_ref=dst, send_sem=send_sem, recv_sem=recv_sem,
            device_id=to, device_id_type=MESH)

    def rows_of(piece, owner):
        return pl.ds(pl.multiple_of((piece * 2 + owner) * ROWS, ROWS), ROWS)

    def piece_of(xs, ys, zs):
        return ((ys % 2) * 4 + zs) * 8 + xs * 2 + ys // 2

    def w_send(piece, to, sem):
        ref = wbuf.at[:, rows_of(piece, core), :]
        copy(ref, ref, send.at[sem], wsem.at[piece], to).start()

    def w_sib(piece, group):
        ref = wbuf.at[:, rows_of(piece, core), :]
        copy(ref, ref, send.at[2], sibsem.at[group], sibling).start()

    def w_wait(piece):
        ref = wbuf.at[:, rows_of(piece, core), :]
        copy(ref, ref, send.at[0], wsem.at[piece], sibling).wait_recv()

    def sib_wait(hop, half):
        ref = wbuf.at[:, pl.ds(0, 8 * ROWS), :]
        copy(ref, ref, send.at[2], sibsem.at[2 * hop + half], sibling).wait_recv()

    def block(xs, yh, ks):
        return xs * 4 + yh * 2 + ks

    def h_ref(b, r):
        return hbuf.at[b, pl.ds(*ROUNDS[r]), :]

    def h_sem(b, r):
        return hsem.at[b * len(ROUNDS) + r]

    def h_send(b, r, to, sem):
        copy(h_ref(b, r), h_ref(b, r), send.at[sem], h_sem(b, r), to).start()

    def h_x(b, r):
        for side in (1, -1):
            h_send(b, r, x_to[side], 3)

    def h_y(b, r):
        for side in (1, -1):
            h_send(b, r, y_to[side], 4)

    def pass_on(to, sem, side, b, r):
        h_send(b, r, to[side], sem)

    def h_wait(b, r):
        copy(h_ref(b, r), h_ref(b, r), send.at[3], h_sem(b, r), sibling).wait_recv()

    own_block = block(x, y_hi, core)
    own_piece = piece_of(x, y, z)
    my_group = x * 4 + y

    def local_hidden(r):
        rows = pl.ds(*ROUNDS[r])
        return pltpu.make_async_copy(hidden.at[rows, :], h_ref(own_block, r),
                                     h_sem(own_block, r))

    def local_weights(part):
        return pltpu.make_async_copy(
            weights.at[:, pl.ds(pl.multiple_of(part * D + my_group * WIDTH, WIDTH), WIDTH)],
            wbuf.at[part, rows_of(own_piece, core), :], misc.at[2 + part])

    for part in range(3):
        local_weights(part).start()

    @pl.when(across == 0)
    def _():
        for r in range(len(ROUNDS)):
            local_hidden(r).start()

    prod[0:8, :] = jnp.zeros((8, WIDTH), jnp.float32)

    barrier = pltpu.get_barrier_semaphore()
    greeted = [device(mx, my, z, core) for mx, my in mates_to[1:]]
    greeted += [z_to[1], z_to[-1], sibling, partner,
                device(x, y, above, 1 - core), device(x, y, below, 1 - core)]
    for to in greeted:
        pl.semaphore_signal(barrier, inc=1, device_id=to, device_id_type=MESH)
    pl.semaphore_wait(barrier, len(greeted))

    def all_to_all(i):
        mx, my = mates_to[i]
        for part in range(3):
            columns = pl.ds(pl.multiple_of(part * D + (mx * 4 + my) * WIDTH, WIDTH), WIDTH)
            copy(weights.at[:, columns], wbuf.at[part, rows_of(own_piece, core), :],
                 send.at[0], wsem.at[own_piece], device(mx, my, z, core)).start()

    @pl.when(across == 1)
    def _():
        for r in range(len(ROUNDS)):
            rows = pl.ds(*ROUNDS[r])
            copy(hidden.at[rows, :], h_ref(own_block, r), send.at[5],
                 h_sem(own_block, r), sibling).start()

    def own_weights(i):
        mx, my = mates[i]
        piece = piece_of(mx, my, z)
        if i == 0:
            for part in range(3):
                local_weights(part).wait()
        else:
            w_wait(piece)
        w_send(piece, z_to[1], 1)
        w_send(piece, z_to[-1], 1)
        w_sib(piece, ORDER[i][1] % 2)

    def near_weights(i):
        mx, my = mates[i]
        piece = piece_of(mx, my, below)
        w_wait(piece)
        if i % 2 == 0:
            w_send(piece, z_to[1], 1)
        w_sib(piece, 6 + ORDER[i][1] % 2)
        piece = piece_of(mx, my, above)
        w_wait(piece)
        if i % 2 == 1:
            w_send(piece, z_to[-1], 1)
        w_sib(piece, 2 + ORDER[i][1] % 2)

    def far_weights(i):
        mx, my = mates[i]
        piece = piece_of(mx, my, (z + 2) % 4)
        w_wait(piece)
        w_sib(piece, 4 + ORDER[i][1] % 2)

    yh_down, yh_up = down // 2, up // 2

    def hidden0(r):
        @pl.when(across == 0)
        def _():
            a, b = block(x, y_hi, 0), block(x, y_hi, 1)
            h_wait(a, r)
            h_x(a, r)
            h_wait(b, r)
            h_y(b, r)

    def hidden0b(r):
        @pl.when(across == 0)
        def _():
            h_y(block(x, y_hi, 0), r)
            h_x(block(x, y_hi, 1), r)

    def hidden1(r):
        @pl.when(across == 0)
        def _():
            a = block(left, y_hi, 0)
            h_wait(a, r)
            if r % 2 == 0:
                pass_on(x_to, 3, 1, a, r)
            h_y(a, r)
            a = block(right, y_hi, 0)
            h_wait(a, r)
            if r % 2 == 1:
                pass_on(x_to, 3, -1, a, r)
            h_y(a, r)

        @pl.when(across == 1)
        def _():
            b = block(x, yh_down, 1)
            h_wait(b, r)
            if r % 2 == 0:
                pass_on(y_to, 4, 1, b, r)
            h_x(b, r)
            b = block(x, yh_up, 1)
            h_wait(b, r)
            if r % 2 == 1:
                pass_on(y_to, 4, -1, b, r)
            h_x(b, r)

    def hidden2(r):
        @pl.when(across == 0)
        def _():
            a = block((x + 2) % 4, y_hi, 0)
            h_wait(a, r)
            h_y(a, r)
            b = block(x, 1 - y_hi, 1)
            h_wait(b, r)
            h_x(b, r)

    xs_steps = (x, left, right, (x + 2) % 4)

    def hidden3a(m, r):
        @pl.when(across == 1)
        def _():
            a = block(xs_steps[m], yh_down, 0)
            h_wait(a, r)
            if (m + r) % 2 == 0:
                pass_on(y_to, 4, 1, a, r)
            a = block(xs_steps[m], yh_up, 0)
            h_wait(a, r)
            if (m + r) % 2 == 1:
                pass_on(y_to, 4, -1, a, r)

    def hidden3b(r):
        for yh in range(2):
            b = block(left, yh, 1)
            h_wait(b, r)
            if (yh + r) % 2 == 0:
                pass_on(x_to, 3, 1, b, r)
            b = block(right, yh, 1)
            h_wait(b, r)
            if (yh + r) % 2 == 1:
                pass_on(x_to, 3, -1, b, r)

    def hidden4a(m, r):
        @pl.when(across == 0)
        def _():
            h_wait(block(xs_steps[m], 1 - y_hi, 0), r)

    def hidden4b(r):
        for yh in range(2):
            h_wait(block((x + 2) % 4, yh, 1), r)

    def make_taps():
        bank8[0:TAPS, :] = bank[...]
        bank8[TAPS:, :] = jnp.zeros((8 - TAPS, FILTERS), jnp.float32)

        @pl.when(across == 0)
        def _():
            groups = WIDTH // GROUP
            filters = lax.broadcasted_iota(jnp.int32, (FILTERS, groups), 0)
            selector = (filters == assigned[...]).astype(jnp.float32)
            picked = jnp.dot(bank8[...], selector, precision=lax.Precision.HIGHEST,
                             preferred_element_type=jnp.float32)
            owner = lax.broadcasted_iota(jnp.int32, (groups, WIDTH), 1) // GROUP
            member = lax.broadcasted_iota(jnp.int32, (groups, WIDTH), 0)
            taps[...] = jnp.dot(picked, (owner == member).astype(jnp.float32),
                                precision=lax.Precision.HIGHEST,
                                preferred_element_type=jnp.float32)
            copy(taps, taps, send.at[6], misc.at[0], sibling).start()

        @pl.when(across == 1)
        def _():
            copy(taps, taps, send.at[6], misc.at[0], sibling).wait_recv()

    codes = [(kind == "x") * 32 + r * 8 + step * 2 + half for kind, r, step, half in DOTS]
    words = [sum(code << 6 * i for i, code in enumerate(codes[first:first + 5]))
             for first in range(0, len(codes), 5)]

    def dot(s):
        word = jnp.int32(words[0])
        for i in range(1, len(words)):
            word = jnp.where(s >= 5 * i, jnp.int32(words[i]), word)
        code = lax.shift_right_logical(word, 6 * (s % 5)) % 64
        by_x, r, step, half = code // 32, code // 8 % 4, code // 2 % 4, code % 2
        z_block = ((y_lo + half) % 2) * 4 + (z + step) % 4
        shift = jnp.where(step == 0, 0, jnp.where(step == 1, 3, step - 1))
        x_block = ((x + shift) % 4) * 2 + half
        b = jnp.where(by_x == 1, x_block, z_block)
        rows = pl.ds(pl.multiple_of((r + 3) % 4 * CHUNK, CHUNK), CHUNK)
        depth = pl.ds(pl.multiple_of(b * 1024, 1024), 1024)
        left_side = jnp.concatenate([hbuf[2 * b, rows, :], hbuf[2 * b + 1, rows, :]], axis=1)
        for part in range(3):
            acc[rows, part * WIDTH:(part + 1) * WIDTH] += jnp.dot(
                left_side, wbuf[part, depth, :], preferred_element_type=jnp.float32)

    SUB = 32

    def products(base):
        def step(i, _):
            rows = pl.ds(pl.multiple_of(base + i * SUB, SUB), SUB)
            prod[pl.ds(pl.multiple_of(base + i * SUB + 8, 8), SUB), :] = (
                acc[rows, WIDTH:2 * WIDTH] * acc[rows, 2 * WIDTH:])
            return 0
        lax.fori_loop(0, CHUNK // SUB, step, 0)

    def filtered(base, count, size):
        def step(i, _):
            first = pl.multiple_of(base + i * size, size)
            near = prod[pl.ds(first, size + 8), :]
            total = jnp.zeros((size, WIDTH), jnp.float32)
            for j in range(TAPS):
                total = total + taps[j:j + 1, :] * near[8 - j:8 - j + size, :]
            rows = pl.ds(first, size)
            stage[rows, :] = (acc[rows, 0:WIDTH] * total).astype(jnp.bfloat16)
            return 0
        lax.fori_loop(0, count, step, 0)

    def out_send(first, count, sem):
        src, dst = stage.at[pl.ds(first, count), :], out.at[pl.ds(first, count), :]

        @pl.when(across == 0)
        def _():
            pltpu.make_async_copy(src, dst, misc.at[sem]).start()

        @pl.when(across == 1)
        def _():
            copy(src, dst, send.at[8], misc.at[sem], partner).start()

    def out_wait(first, count, sem):
        src, dst = stage.at[pl.ds(first, count), :], out.at[pl.ds(first, count), :]

        @pl.when(across == 0)
        def _():
            pltpu.make_async_copy(src, dst, misc.at[sem]).wait()

        @pl.when(across == 1)
        def _():
            copy(src, dst, send.at[8], misc.at[sem], partner).wait_recv()

    halo_from, halo_to = prod.at[pl.ds(TOKENS, 8), :], prod.at[pl.ds(0, 8), :]
    last_window = (z == 3) & (core == 1)
    first_window = (z == 0) & (core == 0)
    next_core = jnp.where(z == 3, 1 - core, core)

    def halo():
        return copy(halo_from, halo_to, send.at[7], misc.at[1], device(x, y, above, next_core))

    def epilogue0():
        products(3 * CHUNK)

        @pl.when(jnp.logical_not(last_window))
        def _():
            halo().start()

        filtered(3 * CHUNK + 32, 7, 32)
        out_send(3 * CHUNK + 32, CHUNK - 32, 5)

    def epilogue1():
        products(0)

        @pl.when(jnp.logical_not(first_window))
        def _():
            halo().wait_recv()

        filtered(0, 8, 32)
        out_send(0, CHUNK, 6)

    def epilogue2():
        products(CHUNK)
        filtered(CHUNK, 8, 32)
        out_send(CHUNK, CHUNK, 7)

    def epilogue3():
        products(2 * CHUNK)
        filtered(2 * CHUNK, 4, 32)
        out_send(2 * CHUNK, 128, 8)
        filtered(2 * CHUNK + 128, 5, 32)
        out_send(2 * CHUNK + 128, 160, 9)

    def zero_acc():
        def step(i, _):
            rows = pl.ds(pl.multiple_of(i * 32, 32), 32)
            acc[rows, :] = jnp.zeros((32, 3 * WIDTH), jnp.float32)
            return 0
        lax.fori_loop(0, TOKENS // 32, step, 0)

    run = {"taps": make_taps, "zero": zero_acc, "all": all_to_all, "own": own_weights, "near": near_weights, "far": far_weights, "sib": sib_wait,
           "h0": hidden0, "h0b": hidden0b, "h1": hidden1, "h2": hidden2, "h3a": hidden3a, "h3b": hidden3b,
           "h4a": hidden4a, "h4b": hidden4b}
    before = timeline()
    last_dot = {r: max(s for s in range(len(DOTS)) if DOTS[s][1] == r) for r in range(CHUNKS)}

    def slot_step(s, _):
        for k in range(len(DOTS)):
            @pl.when(s == k)
            def _(k=k):
                for name, *args in before[k]:
                    run[name](*args)
                for r, epilogue in enumerate((epilogue0, epilogue1, epilogue2)):
                    if k == max(last_dot[i] for i in range(r + 1)) + 1:
                        epilogue()
        dot(s)
        return 0
    lax.fori_loop(0, len(DOTS), slot_step, 0)
    epilogue3()

    out_wait(3 * CHUNK + 32, CHUNK - 32, 5)
    out_wait(0, CHUNK, 6)
    out_wait(CHUNK, CHUNK, 7)
    out_wait(2 * CHUNK, 128, 8)
    out_wait(2 * CHUNK + 128, 160, 9)

    def sent(ref, sem):
        copy(ref, ref, send.at[sem], misc.at[0], sibling).wait_send()

    sent(wbuf.at[:, pl.ds(0, 15 * ROWS), :], 0)
    sent(wbuf.at[:, pl.ds(0, 48 * ROWS), :], 1)
    sent(wbuf.at[:, pl.ds(0, 64 * ROWS), :], 2)

    @pl.when(across == 0)
    def _():
        sent(hbuf.at[pl.ds(0, 9)], 3)
        sent(hbuf.at[pl.ds(0, 10)], 4)
        sent(taps, 6)

    @pl.when(across == 1)
    def _():
        sent(hbuf.at[pl.ds(0, 6)], 3)
        sent(hbuf.at[pl.ds(0, 5)], 4)
        sent(hidden, 5)
        sent(stage, 8)

    @pl.when(jnp.logical_not(last_window))
    def _():
        halo().wait_send()


def on_device(hidden, in_weights, filter_bank, assignment):
    any_space = pl.BlockSpec(memory_space=pl.ANY)
    vmem = pl.BlockSpec(memory_space=pltpu.VMEM)
    return pl.pallas_call(
        kernel,
        name="hyena",
        out_shape=jax.ShapeDtypeStruct((TOKENS, WIDTH), jnp.bfloat16),
        in_specs=[any_space, any_space, vmem, vmem],
        out_specs=any_space,
        scratch_shapes=[
            pltpu.VMEM((16, TOKENS, WIDTH), jnp.bfloat16),
            pltpu.VMEM((3, D, WIDTH), jnp.bfloat16),
            pltpu.VMEM((TOKENS, 3 * WIDTH), jnp.float32),
            pltpu.VMEM((TOKENS + 8, WIDTH), jnp.float32),
            pltpu.VMEM((TOKENS, WIDTH), jnp.bfloat16),
            pltpu.VMEM((8, WIDTH), jnp.float32),
            pltpu.VMEM((8, FILTERS), jnp.float32),
            pltpu.SemaphoreType.DMA((16 * len(ROUNDS),)),
            pltpu.SemaphoreType.DMA((64,)),
            pltpu.SemaphoreType.DMA((8,)),
            pltpu.SemaphoreType.DMA((10,)),
            pltpu.SemaphoreType.DMA((10,)),
        ],
        compiler_params=pltpu.CompilerParams(
            collective_id=0, has_side_effects=True, vmem_limit_bytes=60 * 2**20),
        cost_estimate=pl.CostEstimate(
            flops=2 * TOKENS * D * 3 * WIDTH, bytes_accessed=44 * 2**20, transcendentals=0),
    )(hidden, in_weights, filter_bank, assignment[None, :])


def solution(mesh):
    in_specs = (P("seq", "chan"), P(("seq", "chan"), None), P(), P("chan"))
    return jax.shard_map(
        on_device, mesh=mesh, in_specs=in_specs, out_specs=P("seq", "chan"), check_vma=False)
```

```python
import jax
import jax.numpy as jnp
from jax import lax
from jax.experimental import pallas as pl
from jax.experimental.pallas import tpu as pltpu
from jax.sharding import PartitionSpec as P

D = 8192
GROUP = 16
TAPS = 7
FILTERS = 512
TOKENS = 1024
WIDTH = 512
ROWS = 64
CHUNK = 256
CHUNKS = TOKENS // CHUNK
MESH = pl.DeviceIdType.MESH

ROUNDS = ((768, 256), (0, 256), (256, 256), (512, 256))
ORDER = ((0, 0), (1, 0), (3, 0), (0, 2), (2, 0), (1, 2), (3, 2), (2, 2),
         (0, 1), (0, 3), (1, 1), (3, 3), (1, 3), (3, 1), (2, 1), (2, 3))
STARTS = (19.54, 40.17, 60.8, 81.43)
STAGES = (0.0, 6.54, 23.09, 34.44, 49.63)
LAST = (12.84, 25.44, 35.22, 44.3, 71.25)
SPREAD = (2.51, 2.56)
SPLIT = 21.05
ALL = (0, 0.5)
OWN = (3.64, 1.48)
NEAR = (19.06, 1.08, 5.8)
FAR = (73.66, 4.68)
DOT = 1.7

HOPS = (0, 1, 3, 2)
DOTS = (
    ("z", 0, 0, 0), ("z", 0, 1, 0), ("z", 0, 3, 0), ("z", 1, 0, 0),
    ("z", 1, 1, 0), ("z", 1, 3, 0), ("z", 0, 0, 1), ("z", 0, 1, 1),
    ("z", 0, 3, 1), ("z", 1, 0, 1), ("z", 1, 1, 1), ("z", 1, 3, 1),
    ("z", 0, 2, 0), ("z", 1, 2, 0), ("z", 2, 0, 0), ("z", 2, 0, 1),
    ("z", 2, 1, 0), ("z", 2, 1, 1), ("z", 2, 3, 0), ("z", 2, 3, 1),
    ("z", 2, 2, 0), ("z", 0, 2, 1), ("z", 1, 2, 1), ("z", 2, 2, 1),
    ("x", 3, 0, 1), ("x", 3, 0, 0), ("x", 3, 1, 0), ("x", 3, 1, 1),
    ("x", 3, 2, 0), ("x", 3, 2, 1), ("x", 3, 3, 0), ("x", 3, 3, 1),
)


def hidden_needs(m, r):
    return [("h3a", m, r), ("h4a", m, r)] + [
        [("h1", r), ("h2", r)], [("h1", r), ("h3b", r)], [("h1", r), ("h3b", r)],
        [("h2", r), ("h4b", r)]][m]


def timeline():
    when = {("taps",): 30.0}
    for i in range(16):
        if i:
            when["all", i] = ALL[0] + ALL[1] * i
        when["own", i] = OWN[0] + OWN[1] * i
        when["near", i] = max(NEAR[0], NEAR[1] + NEAR[2] * i)
        when["far", i] = FAR[0] + FAR[1] * (i // 2 + 1)
    for r, start in enumerate(STARTS):
        stages = LAST if r == CHUNKS - 1 else STAGES
        when["h0b", r] = start + stages[0] + SPLIT
        for index in range(3):
            when["h%d" % index, r] = start + stages[index]
        for m in range(4):
            when["h3a", m, r] = start + stages[3] + SPREAD[0] * m
            when["h4a", m, r] = start + stages[4] + SPREAD[1] * m
        when["h3b", r] = start + stages[3] + SPREAD[0] * 1.5
        when["h4b", r] = start + stages[4] + SPREAD[1] * 2.5
    kinds = {0: "own", 1: "near", 3: "near", 2: "far"}
    for hop in HOPS:
        for half in range(2):
            last = max(when[kinds[hop], i] for i in range(16) if ORDER[i][1] % 2 == half)
            when["sib", hop, half] = last + 3.0

    slots, placed, clock = [], set(), 0.0
    names = list(when)
    for kind, r, step, half in DOTS:
        if kind == "z":
            needs = [key for m in range(4) for key in hidden_needs(m, r)]
            needs += [("sib", step, half)]
        else:
            needs = hidden_needs(step, r) + [
                ("sib", hop, h) for hop in HOPS for h in range(2)]
        clock = max([clock + DOT] + [when[key] for key in needs])
        ready = [key for key in names if when[key] <= clock and key not in placed]
        ready = sorted(ready, key=when.get)
        placed.update(ready)
        slots.append(ready)
    rest = [key for key in names if key not in placed]
    assert not rest
    return slots


def device(x, y, z, core):
    return ((y % 2) * 4 + z, x * 4 + (y // 2) * 2 + core)


def kernel(hidden, weights, bank, assigned, out, hbuf, wbuf, acc, prod, stage, taps, bank8,
           hsem, wsem, sibsem, misc, send):
    seq, chan = lax.axis_index("seq"), lax.axis_index("chan")
    x, y, z, core = chan // 4, (chan // 2 % 2) * 2 + seq // 4, seq % 4, chan % 2
    y_hi, y_lo = y // 2, y % 2
    across = (y_lo + core) % 2
    left, right = (x + 3) % 4, (x + 1) % 4
    down, up = (y + 3) % 4, (y + 1) % 4
    below, above = (z + 3) % 4, (z + 1) % 4
    sibling = device(x, y, z, 1 - core)
    partner = device(x, y + 1 - 2 * y_lo, z, 1 - core)
    x_to = {1: device(right, y, z, core), -1: device(left, y, z, core)}
    y_to = {1: device(x, up, z, core), -1: device(x, down, z, core)}
    z_to = {1: device(x, y, above, core), -1: device(x, y, below, core)}

    sign = 1 - 2 * core
    mates_to = [((x + sign * dx + 4) % 4, (y + sign * dy + 4) % 4) for dx, dy in ORDER]
    mates = [((x - sign * dx + 4) % 4, (y - sign * dy + 4) % 4) for dx, dy in ORDER]

    def copy(src, dst, send_sem, recv_sem, to):
        return pltpu.make_async_remote_copy(
            src_ref=src, dst_ref=dst, send_sem=send_sem, recv_sem=recv_sem,
            device_id=to, device_id_type=MESH)

    def rows_of(piece, owner):
        return pl.ds(pl.multiple_of((piece * 2 + owner) * ROWS, ROWS), ROWS)

    def piece_of(xs, ys, zs):
        return ((ys % 2) * 4 + zs) * 8 + xs * 2 + ys // 2

    def w_send(piece, to, sem):
        ref = wbuf.at[:, rows_of(piece, core), :]
        copy(ref, ref, send.at[sem], wsem.at[piece], to).start()

    def w_sib(piece, group):
        ref = wbuf.at[:, rows_of(piece, core), :]
        copy(ref, ref, send.at[2], sibsem.at[group], sibling).start()

    def w_wait(piece):
        ref = wbuf.at[:, rows_of(piece, core), :]
        copy(ref, ref, send.at[0], wsem.at[piece], sibling).wait_recv()

    def sib_wait(hop, half):
        ref = wbuf.at[:, pl.ds(0, 8 * ROWS), :]
        copy(ref, ref, send.at[2], sibsem.at[2 * hop + half], sibling).wait_recv()

    def block(xs, yh, ks):
        return xs * 4 + yh * 2 + ks

    def h_ref(b, r):
        return hbuf.at[b, pl.ds(*ROUNDS[r]), :]

    def h_sem(b, r):
        return hsem.at[b * len(ROUNDS) + r]

    def h_send(b, r, to, sem):
        copy(h_ref(b, r), h_ref(b, r), send.at[sem], h_sem(b, r), to).start()

    def h_x(b, r):
        for side in (1, -1):
            h_send(b, r, x_to[side], 3)

    def h_y(b, r):
        for side in (1, -1):
            h_send(b, r, y_to[side], 4)

    def pass_on(to, sem, side, b, r):
        h_send(b, r, to[side], sem)

    def h_wait(b, r):
        copy(h_ref(b, r), h_ref(b, r), send.at[3], h_sem(b, r), sibling).wait_recv()

    own_block = block(x, y_hi, core)
    own_piece = piece_of(x, y, z)
    my_group = x * 4 + y

    def local_hidden(r):
        rows = pl.ds(*ROUNDS[r])
        return pltpu.make_async_copy(hidden.at[rows, :], h_ref(own_block, r),
                                     h_sem(own_block, r))

    def local_weights(part):
        return pltpu.make_async_copy(
            weights.at[:, pl.ds(pl.multiple_of(part * D + my_group * WIDTH, WIDTH), WIDTH)],
            wbuf.at[part, rows_of(own_piece, core), :], misc.at[2 + part])

    for part in range(3):
        local_weights(part).start()

    @pl.when(across == 0)
    def _():
        for r in range(len(ROUNDS)):
            local_hidden(r).start()

    prod[0:8, :] = jnp.zeros((8, WIDTH), jnp.float32)

    def pick_taps():
        bank8[0:TAPS, :] = bank[...]
        bank8[TAPS:, :] = jnp.zeros((8 - TAPS, FILTERS), jnp.float32)

        @pl.when(across == 0)
        def _():
            groups = WIDTH // GROUP
            filters = lax.broadcasted_iota(jnp.int32, (FILTERS, groups), 0)
            selector = (filters == assigned[...]).astype(jnp.float32)
            picked = jnp.dot(bank8[...], selector, precision=lax.Precision.HIGHEST,
                             preferred_element_type=jnp.float32)
            owner = lax.broadcasted_iota(jnp.int32, (groups, WIDTH), 1) // GROUP
            member = lax.broadcasted_iota(jnp.int32, (groups, WIDTH), 0)
            taps[...] = jnp.dot(picked, (owner == member).astype(jnp.float32),
                                precision=lax.Precision.HIGHEST,
                                preferred_element_type=jnp.float32)

    def zero_acc():
        def step(i, _):
            rows = pl.ds(pl.multiple_of(i * 32, 32), 32)
            acc[rows, :] = jnp.zeros((32, 3 * WIDTH), jnp.float32)
            return 0
        lax.fori_loop(0, TOKENS // 32, step, 0)

    barrier = pltpu.get_barrier_semaphore()
    greeted = [device(mx, my, z, core) for mx, my in mates_to[1:]]
    greeted += [z_to[1], z_to[-1], sibling, partner,
                device(x, y, above, 1 - core), device(x, y, below, 1 - core)]
    for to in greeted:
        pl.semaphore_signal(barrier, inc=1, device_id=to, device_id_type=MESH)
    zero_acc()
    pick_taps()
    pl.semaphore_wait(barrier, len(greeted))

    def all_to_all(i):
        mx, my = mates_to[i]
        for part in range(3):
            columns = pl.ds(pl.multiple_of(part * D + (mx * 4 + my) * WIDTH, WIDTH), WIDTH)
            copy(weights.at[:, columns], wbuf.at[part, rows_of(own_piece, core), :],
                 send.at[0], wsem.at[own_piece], device(mx, my, z, core)).start()

    @pl.when(across == 1)
    def _():
        for r in range(len(ROUNDS)):
            rows = pl.ds(*ROUNDS[r])
            copy(hidden.at[rows, :], h_ref(own_block, r), send.at[5],
                 h_sem(own_block, r), sibling).start()

    def own_weights(i):
        mx, my = mates[i]
        piece = piece_of(mx, my, z)
        if i == 0:
            for part in range(3):
                local_weights(part).wait()
        else:
            w_wait(piece)
        w_send(piece, z_to[1], 1)
        w_send(piece, z_to[-1], 1)
        w_sib(piece, ORDER[i][1] % 2)

    def near_weights(i):
        mx, my = mates[i]
        piece = piece_of(mx, my, below)
        w_wait(piece)
        if i % 2 == 0:
            w_send(piece, z_to[1], 1)
        w_sib(piece, 6 + ORDER[i][1] % 2)
        piece = piece_of(mx, my, above)
        w_wait(piece)
        if i % 2 == 1:
            w_send(piece, z_to[-1], 1)
        w_sib(piece, 2 + ORDER[i][1] % 2)

    def far_weights(i):
        mx, my = mates[i]
        piece = piece_of(mx, my, (z + 2) % 4)
        w_wait(piece)
        w_sib(piece, 4 + ORDER[i][1] % 2)

    yh_down, yh_up = down // 2, up // 2

    def hidden0(r):
        @pl.when(across == 0)
        def _():
            a, b = block(x, y_hi, 0), block(x, y_hi, 1)
            h_wait(a, r)
            h_x(a, r)
            h_wait(b, r)
            h_y(b, r)

    def hidden0b(r):
        @pl.when(across == 0)
        def _():
            h_y(block(x, y_hi, 0), r)
            h_x(block(x, y_hi, 1), r)

    def hidden1(r):
        @pl.when(across == 0)
        def _():
            a = block(left, y_hi, 0)
            h_wait(a, r)
            if r % 2 == 0:
                pass_on(x_to, 3, 1, a, r)
            h_y(a, r)
            a = block(right, y_hi, 0)
            h_wait(a, r)
            if r % 2 == 1:
                pass_on(x_to, 3, -1, a, r)
            h_y(a, r)

        @pl.when(across == 1)
        def _():
            b = block(x, yh_down, 1)
            h_wait(b, r)
            if r % 2 == 0:
                pass_on(y_to, 4, 1, b, r)
            h_x(b, r)
            b = block(x, yh_up, 1)
            h_wait(b, r)
            if r % 2 == 1:
                pass_on(y_to, 4, -1, b, r)
            h_x(b, r)

    def hidden2(r):
        @pl.when(across == 0)
        def _():
            a = block((x + 2) % 4, y_hi, 0)
            h_wait(a, r)
            h_y(a, r)
            b = block(x, 1 - y_hi, 1)
            h_wait(b, r)
            h_x(b, r)

    xs_steps = (x, left, right, (x + 2) % 4)

    def hidden3a(m, r):
        @pl.when(across == 1)
        def _():
            a = block(xs_steps[m], yh_down, 0)
            h_wait(a, r)
            if (m + r) % 2 == 0:
                pass_on(y_to, 4, 1, a, r)
            a = block(xs_steps[m], yh_up, 0)
            h_wait(a, r)
            if (m + r) % 2 == 1:
                pass_on(y_to, 4, -1, a, r)

    def hidden3b(r):
        for yh in range(2):
            b = block(left, yh, 1)
            h_wait(b, r)
            if (yh + r) % 2 == 0:
                pass_on(x_to, 3, 1, b, r)
            b = block(right, yh, 1)
            h_wait(b, r)
            if (yh + r) % 2 == 1:
                pass_on(x_to, 3, -1, b, r)

    def hidden4a(m, r):
        @pl.when(across == 0)
        def _():
            h_wait(block(xs_steps[m], 1 - y_hi, 0), r)

    def hidden4b(r):
        for yh in range(2):
            h_wait(block((x + 2) % 4, yh, 1), r)

    def share_taps():
        @pl.when(across == 0)
        def _():
            copy(taps, taps, send.at[6], misc.at[0], sibling).start()

        @pl.when(across == 1)
        def _():
            copy(taps, taps, send.at[6], misc.at[0], sibling).wait_recv()

    codes = [(kind == "x") * 32 + r * 8 + step * 2 + half for kind, r, step, half in DOTS]
    words = [sum(code << 6 * i for i, code in enumerate(codes[first:first + 5]))
             for first in range(0, len(codes), 5)]

    def dot(s):
        word = jnp.int32(words[0])
        for i in range(1, len(words)):
            word = jnp.where(s >= 5 * i, jnp.int32(words[i]), word)
        code = lax.shift_right_logical(word, 6 * (s % 5)) % 64
        by_x, r, step, half = code // 32, code // 8 % 4, code // 2 % 4, code % 2
        z_block = ((y_lo + half) % 2) * 4 + (z + step) % 4
        shift = jnp.where(step == 0, 0, jnp.where(step == 1, 3, step - 1))
        x_block = ((x + shift) % 4) * 2 + half
        b = jnp.where(by_x == 1, x_block, z_block)
        rows = pl.ds(pl.multiple_of((r + 3) % 4 * CHUNK, CHUNK), CHUNK)
        depth = pl.ds(pl.multiple_of(b * 1024, 1024), 1024)
        left_side = jnp.concatenate([hbuf[2 * b, rows, :], hbuf[2 * b + 1, rows, :]], axis=1)
        for part in range(3):
            acc[rows, part * WIDTH:(part + 1) * WIDTH] += jnp.dot(
                left_side, wbuf[part, depth, :], preferred_element_type=jnp.float32)

    SUB = 32

    def products(base):
        def step(i, _):
            rows = pl.ds(pl.multiple_of(base + i * SUB, SUB), SUB)
            prod[pl.ds(pl.multiple_of(base + i * SUB + 8, 8), SUB), :] = (
                acc[rows, WIDTH:2 * WIDTH] * acc[rows, 2 * WIDTH:])
            return 0
        lax.fori_loop(0, CHUNK // SUB, step, 0)

    def filtered(base, count, size):
        def step(i, _):
            first = pl.multiple_of(base + i * size, size)
            near = prod[pl.ds(first, size + 8), :]
            total = jnp.zeros((size, WIDTH), jnp.float32)
            for j in range(TAPS):
                total = total + taps[j:j + 1, :] * near[8 - j:8 - j + size, :]
            rows = pl.ds(first, size)
            stage[rows, :] = (acc[rows, 0:WIDTH] * total).astype(jnp.bfloat16)
            return 0
        lax.fori_loop(0, count, step, 0)

    def out_send(first, count, sem):
        src, dst = stage.at[pl.ds(first, count), :], out.at[pl.ds(first, count), :]

        @pl.when(across == 0)
        def _():
            pltpu.make_async_copy(src, dst, misc.at[sem]).start()

        @pl.when(across == 1)
        def _():
            copy(src, dst, send.at[8], misc.at[sem], partner).start()

    def out_wait(first, count, sem):
        src, dst = stage.at[pl.ds(first, count), :], out.at[pl.ds(first, count), :]

        @pl.when(across == 0)
        def _():
            pltpu.make_async_copy(src, dst, misc.at[sem]).wait()

        @pl.when(across == 1)
        def _():
            copy(src, dst, send.at[8], misc.at[sem], partner).wait_recv()

    halo_from, halo_to = prod.at[pl.ds(TOKENS, 8), :], prod.at[pl.ds(0, 8), :]
    last_window = (z == 3) & (core == 1)
    first_window = (z == 0) & (core == 0)
    next_core = jnp.where(z == 3, 1 - core, core)

    def halo():
        return copy(halo_from, halo_to, send.at[7], misc.at[1], device(x, y, above, next_core))

    def epilogue0():
        products(3 * CHUNK)

        @pl.when(jnp.logical_not(last_window))
        def _():
            halo().start()

        filtered(3 * CHUNK + 32, 7, 32)
        out_send(3 * CHUNK + 32, CHUNK - 32, 5)

    def epilogue1():
        products(0)

        @pl.when(jnp.logical_not(first_window))
        def _():
            halo().wait_recv()

        filtered(0, 8, 32)
        out_send(0, CHUNK, 6)

    def epilogue2():
        products(CHUNK)
        filtered(CHUNK, 8, 32)
        out_send(CHUNK, CHUNK, 7)

    def epilogue3():
        products(2 * CHUNK)
        filtered(2 * CHUNK, 4, 32)
        out_send(2 * CHUNK, 128, 8)
        filtered(2 * CHUNK + 128, 5, 32)
        out_send(2 * CHUNK + 128, 160, 9)

    run = {"taps": share_taps, "all": all_to_all, "own": own_weights, "near": near_weights, "far": far_weights, "sib": sib_wait,
           "h0": hidden0, "h0b": hidden0b, "h1": hidden1, "h2": hidden2, "h3a": hidden3a, "h3b": hidden3b,
           "h4a": hidden4a, "h4b": hidden4b}
    before = timeline()
    last_dot = {r: max(s for s in range(len(DOTS)) if DOTS[s][1] == r) for r in range(CHUNKS)}

    def slot_step(s, _):
        for k in range(len(DOTS)):
            @pl.when(s == k)
            def _(k=k):
                for name, *args in before[k]:
                    run[name](*args)
                for r, epilogue in enumerate((epilogue0, epilogue1, epilogue2)):
                    if k == max(last_dot[i] for i in range(r + 1)) + 1:
                        epilogue()
        dot(s)
        return 0
    lax.fori_loop(0, len(DOTS), slot_step, 0)
    epilogue3()

    out_wait(3 * CHUNK + 32, CHUNK - 32, 5)
    out_wait(0, CHUNK, 6)
    out_wait(CHUNK, CHUNK, 7)
    out_wait(2 * CHUNK, 128, 8)
    out_wait(2 * CHUNK + 128, 160, 9)

    def sent(ref, sem):
        copy(ref, ref, send.at[sem], misc.at[0], sibling).wait_send()

    sent(wbuf.at[:, pl.ds(0, 15 * ROWS), :], 0)
    sent(wbuf.at[:, pl.ds(0, 48 * ROWS), :], 1)
    sent(wbuf.at[:, pl.ds(0, 64 * ROWS), :], 2)

    @pl.when(across == 0)
    def _():
        sent(hbuf.at[pl.ds(0, 9)], 3)
        sent(hbuf.at[pl.ds(0, 10)], 4)
        sent(taps, 6)

    @pl.when(across == 1)
    def _():
        sent(hbuf.at[pl.ds(0, 6)], 3)
        sent(hbuf.at[pl.ds(0, 5)], 4)
        sent(hidden, 5)
        sent(stage, 8)

    @pl.when(jnp.logical_not(last_window))
    def _():
        halo().wait_send()


def on_device(hidden, in_weights, filter_bank, assignment):
    any_space = pl.BlockSpec(memory_space=pl.ANY)
    vmem = pl.BlockSpec(memory_space=pltpu.VMEM)
    return pl.pallas_call(
        kernel,
        name="hyena",
        out_shape=jax.ShapeDtypeStruct((TOKENS, WIDTH), jnp.bfloat16),
        in_specs=[any_space, any_space, vmem, vmem],
        out_specs=any_space,
        scratch_shapes=[
            pltpu.VMEM((16, TOKENS, WIDTH), jnp.bfloat16),
            pltpu.VMEM((3, D, WIDTH), jnp.bfloat16),
            pltpu.VMEM((TOKENS, 3 * WIDTH), jnp.float32),
            pltpu.VMEM((TOKENS + 8, WIDTH), jnp.float32),
            pltpu.VMEM((TOKENS, WIDTH), jnp.bfloat16),
            pltpu.VMEM((8, WIDTH), jnp.float32),
            pltpu.VMEM((8, FILTERS), jnp.float32),
            pltpu.SemaphoreType.DMA((16 * len(ROUNDS),)),
            pltpu.SemaphoreType.DMA((64,)),
            pltpu.SemaphoreType.DMA((8,)),
            pltpu.SemaphoreType.DMA((10,)),
            pltpu.SemaphoreType.DMA((10,)),
        ],
        compiler_params=pltpu.CompilerParams(
            collective_id=0, has_side_effects=True, vmem_limit_bytes=60 * 2**20),
        cost_estimate=pl.CostEstimate(
            flops=2 * TOKENS * D * 3 * WIDTH, bytes_accessed=44 * 2**20, transcendentals=0),
    )(hidden, in_weights, filter_bank, assignment[None, :])


def solution(mesh):
    in_specs = (P("seq", "chan"), P(("seq", "chan"), None), P(), P("chan"))
    return jax.shard_map(
        on_device, mesh=mesh, in_specs=in_specs, out_specs=P("seq", "chan"), check_vma=False)
```
